32 devices in a mesh: expert: 8 (over y, x, core), ffn: 4 (over z).
Axes of the slice: x: 2, y: 2, z: 4, core: 2. Of those that a mesh axis runs over, the one named last changes fastest.
Arguments:
- tokens: bfloat16 [512, 4096], P('expert', 'ffn'), may hold values from -6 to 6
- cotangent: bfloat16 [512, 4096], P('expert', 'ffn'), may hold values from -6 to 6
- route_ids: int32 [512, 4], P('expert'), may hold values from 0 to 7, all different within a row; in each aligned block of 64 rows (0 to 63, 64 to 127, ...) at most 48 rows name the same one
- route_weights: bfloat16 [512, 4], P('expert'), may hold values from 0.019897461 to 0.5
- gate_weight: bfloat16 [8, 4096, 1024], P('expert', None, 'ffn'), may hold values from -0.09375 to 0.09375
- up_weight: bfloat16 [8, 4096, 1024], P('expert', None, 'ffn'), may hold values from -0.09375 to 0.09375
- down_weight: bfloat16 [8, 1024, 4096], P('expert', 'ffn'), may hold values from -0.1875 to 0.1875
- fisher: float32 [8, 1024, 4096], P('expert', 'ffn'), may hold values from 20 to 400
- anchor: float32 [8, 1024, 4096], P('expert', 'ffn'), may hold values from -0.18 to 0.18
Outputs:
- grad_tokens: bfloat16 [512, 4096], P('expert', 'ffn')
- grad_route_weights: float32 [512, 4], P('expert')
- grad_gate: bfloat16 [8, 4096, 1024], P('expert', None, 'ffn')
- grad_up: bfloat16 [8, 4096, 1024], P('expert', None, 'ffn')
- grad_down: bfloat16 [8, 1024, 4096], P('expert', 'ffn')
The draws below stay inside these ranges and needn't reach their ends.
Inputs may be any that keep to these rules, and one draw needn't show every extreme that they name: `route_ids`: each row names 4 different experts. Among the 64 rows of one index of expert, no expert is named more than 48 times, a bound that some block reaches.
All inputs are finite; a program needn't handle non-finite values.
Results may differ from the reference program's by a relative error of at most 0.005.
Values may be sent and summed in bfloat16 or wider, within the bound.
No kernel may reach another device: no remote copies, remote signals or barrier semaphores. Data moves between devices by JAX's collectives and lax.ppermute only.
A program may use at most 128 MiB of HBM per device.

```python
import math
import jax
import jax.numpy as jnp
import numpy as np
from jax import lax

D = 4096
FF = 1024
TOK = 64
EXPERTS = 8
TOPK = 4
CAP = 48
TOKENS = 512
N_EXPERT = 8


def steps_of(own_key, dims, cuts, least, top_value):
    gain = 1.0
    for axis_at, blocks in cuts:
        draws = jax.random.uniform(jax.random.fold_in(jax.random.fold_in(own_key, 6), axis_at), (blocks,), jnp.float32, least / len(cuts), top_value / len(cuts))
        gain = gain * jnp.repeat(jnp.exp(draws), dims[axis_at] // blocks).reshape((-1,) + (1,) * (len(dims) - 1 - axis_at))
    return gain


def assign_block(key, own, number, rows, amount, top, bound, skew):
    sequence = jax.random.permutation(key, amount)
    heavy_load, common = shares(amount, rows * top, bound, skew, True), shares(amount, rows * top, bound, skew, False)
    places = jnp.arange(amount)

    def named(lengths, turn):
        used = int((lengths > 0).sum())
        fixed = max(1, used // 4)
        moved = fixed + (places - fixed + turn * (used - fixed)) % max(1, amount - fixed)
        return jnp.zeros((amount,), jnp.int32).at[sequence[jnp.where(places < fixed, places, moved)]].set(jnp.asarray(lengths, jnp.int32))

    lengths = jnp.where(number % 4 == 0, named(heavy_load, number // 4), named(common, number - number // 4 - 1))
    mixed = jax.random.permutation(jax.random.fold_in(own, 3), amount)
    giver, receiver = mixed[0:amount // 2 * 2:2], mixed[1:amount // 2 * 2:2]
    room = jnp.minimum(lengths[giver] - 1, bound - lengths[receiver]) // 2
    room = jnp.where((giver == sequence[0]) | (receiver == sequence[0]) | (lengths[receiver] == 0), 0, jnp.maximum(room, 0))
    moved = jax.random.randint(jax.random.fold_in(own, 4), (amount // 2,), 0, 1 << 20) % (room + 1)
    lengths = lengths.at[giver].add(-moved).at[receiver].add(moved)
    items = jnp.searchsorted(jnp.cumsum(lengths), jnp.arange(rows * top), side="right").astype(jnp.int32)
    listing = items.reshape(top, rows).T
    listing = listing[jax.random.permutation(jax.random.fold_in(own, 1), rows)]
    turn = jax.random.randint(jax.random.fold_in(own, 2), (rows, 1), 0, top)
    return jnp.take_along_axis(listing, (jnp.arange(top)[None, :] + turn) % top, axis=1)


def shares(number_of, total, most, slope, full):
    loads = [(1 << 20) // math.isqrt(rank ** slope) + 1 for rank in range(1, number_of + 1)]
    largest = most if full else min(most, max(-(-total // number_of), total * loads[0] // sum(loads)))
    least = 1 if total - largest >= number_of - 1 else 0
    given, spare = [largest] + [least] * (number_of - 1), total - largest - least * (number_of - 1)
    while spare > 0:
        candidates = [i for i in range(1, number_of) if given[i] < largest] or [i for i in range(1, number_of) if given[i] < most]
        pool, left = sum([loads[i] for i in candidates]), spare
        for i in candidates:
            extra = min(most - given[i], max(1, left * loads[i] // pool), spare)
            given[i] = given[i] + extra
            spare = spare - extra
    return np.array(given)


def centred(key, dims, spread, most, cuts=(), kind=jnp.bfloat16):
    entries = jax.random.normal(key, dims, jnp.float32) * spread
    if len(cuts) > 0:
        entries = steps_of(key, dims, cuts, -0.22, 0.18) * entries
    return jnp.clip(entries, min=-most, max=most).astype(kind)


def setup_inputs(seed: int = 0) -> dict:
    arg_keys = jax.random.split(jax.random.key(seed), 10)
    tokens = centred(arg_keys[0], (TOKENS, D), 1.0, 6.0, ((0, 8), (1, 4)))
    cotangent = centred(arg_keys[1], (TOKENS, D), 1.0, 6.0, ((0, 8), (1, 4)))
    route_ids_keys = jax.random.split(jax.random.fold_in(arg_keys[2], 1), TOKENS // TOK)
    route_ids_turns = jax.random.permutation(jax.random.fold_in(arg_keys[2], 3), TOKENS // TOK)
    route_ids = jax.vmap(lambda own, number: assign_block(jax.random.fold_in(arg_keys[2], 2), own, number, TOK, EXPERTS, TOPK, CAP, 2))(route_ids_keys, route_ids_turns).reshape((TOKENS, TOPK))
    route_weights = jnp.clip(jnp.exp(math.log(0.5) - 3.224016 * jax.random.uniform(arg_keys[3], (TOKENS, TOPK), jnp.float32) ** steps_of(arg_keys[3], (TOKENS, TOPK), ((0, 8),), -0.2, 0.2)), 0.019897461, 0.5).astype(jnp.bfloat16)
    gate_weight = centred(arg_keys[4], (EXPERTS, D, FF), D ** -0.5, 0.09375, ((0, 8), (2, 4)))
    up_weight = centred(arg_keys[5], (EXPERTS, D, FF), D ** -0.5, 0.09375, ((0, 8), (2, 4)))
    down_weight = centred(arg_keys[6], (EXPERTS, FF, D), FF ** -0.5, 0.1875, ((0, 8), (1, 4)))
    fisher = jnp.clip(jnp.exp(math.log(400.0) - 2.9957323 * jax.random.uniform(arg_keys[7], (EXPERTS, FF, D), jnp.float32) ** steps_of(arg_keys[7], (EXPERTS, FF, D), ((0, 8), (1, 4)), -0.2, 0.2)), 20.0, 400.0)
    anchor = centred(arg_keys[8], (EXPERTS, FF, D), 0.03, 0.18, ((0, 8), (1, 4)), jnp.float32)
    return {"tokens": tokens, "cotangent": cotangent, "route_ids": route_ids, "route_weights": route_weights, "gate_weight": gate_weight, "up_weight": up_weight, "down_weight": down_weight, "fisher": fisher, "anchor": anchor}


def expert_pass(rows_x, rows_dy, rows_w, gate_part, up_part, down_part, fisher_part, anchor_part):
    gate_pre = jnp.dot(rows_x, gate_part, preferred_element_type=jnp.float32)
    up_pre = jnp.dot(rows_x, up_part, preferred_element_type=jnp.float32)
    logistic = jax.nn.sigmoid(gate_pre)
    active = gate_pre * logistic
    hidden = active * up_pre
    back = lax.dot_general(rows_dy, down_part, (((1,), (1,)), ((), ())), preferred_element_type=jnp.float32)
    route_part = jnp.sum(back * hidden, axis=1)
    weight_col = rows_w.astype(jnp.float32)[:, None]
    scaled = weight_col * back
    grad_pre_gate = (scaled * up_pre * logistic * (1.0 + gate_pre * (1.0 - logistic))).astype(jnp.bfloat16)
    grad_pre_up = (scaled * active).astype(jnp.bfloat16)
    weighted = (weight_col * hidden).astype(jnp.bfloat16)
    over_rows = (((0,), (0,)), ((), ()))
    grad_gate = lax.dot_general(rows_x, grad_pre_gate, over_rows, preferred_element_type=jnp.float32).astype(jnp.bfloat16)
    grad_up = lax.dot_general(rows_x, grad_pre_up, over_rows, preferred_element_type=jnp.float32).astype(jnp.bfloat16)
    down_data = lax.dot_general(weighted, rows_dy, over_rows, preferred_element_type=jnp.float32)
    grad_down = (down_data + fisher_part * (down_part.astype(jnp.float32) - anchor_part)).astype(jnp.bfloat16)
    over_units = (((1,), (1,)), ((), ()))
    feature_part = lax.dot_general(grad_pre_gate, gate_part, over_units, preferred_element_type=jnp.float32)
    feature_part = feature_part + lax.dot_general(grad_pre_up, up_part, over_units, preferred_element_type=jnp.float32)
    return route_part, feature_part, grad_gate, grad_up, grad_down


def reference(tokens, cotangent, route_ids, route_weights, gate_weight, up_weight, down_weight, fisher, anchor):
    token_total = tokens.shape[0]
    row_limit = N_EXPERT * CAP
    order_base = jnp.arange(token_total, dtype=jnp.int32)

    def one_expert(carry, items):
        grad_acc, route_acc = carry
        expert, gate_part, up_part, down_part, fisher_part, anchor_part = items
        chosen = route_ids == expert
        routed = jnp.any(chosen, axis=1)
        weight_tok = jnp.sum(jnp.where(chosen, route_weights, jnp.zeros_like(route_weights)), axis=1).astype(jnp.bfloat16)
        keys = jnp.where(routed, order_base, order_base + token_total)
        picked = jnp.argsort(keys)[:row_limit].astype(jnp.int32)
        live = routed[picked]
        rows_w = jnp.where(live, weight_tok[picked], jnp.zeros((row_limit,), jnp.bfloat16))
        route_part, feature_part, grad_gate, grad_up, grad_down = expert_pass(
            tokens[picked], cotangent[picked], rows_w, gate_part, up_part, down_part, fisher_part, anchor_part)
        live_f = live.astype(jnp.float32)
        grad_acc = grad_acc.at[picked].add(feature_part * live_f[:, None])
        route_tok = jnp.zeros((token_total,), jnp.float32).at[picked].add(route_part * live_f)
        route_acc = route_acc + jnp.where(chosen, route_tok[:, None], jnp.zeros_like(route_acc))
        return (grad_acc, route_acc), (grad_gate, grad_up, grad_down)

    start = (jnp.zeros(tokens.shape, jnp.float32), jnp.zeros(route_ids.shape, jnp.float32))
    expert_ids = jnp.arange(EXPERTS, dtype=jnp.int32)
    (grad_acc, route_acc), (grads_gate, grads_up, grads_down) = lax.scan(
        one_expert, start, (expert_ids, gate_weight, up_weight, down_weight, fisher, anchor))
    return grad_acc.astype(jnp.bfloat16), route_acc, grads_gate, grads_up, grads_down
```

```python
import functools

import jax
import jax.numpy as jnp
from jax import lax
from jax.experimental import pallas as pl
from jax.experimental.pallas import tpu as pltpu
from jax.sharding import PartitionSpec as P

BF = jnp.bfloat16
F32 = jnp.float32
LANES = 128
VMEM_LIMIT = 56 * 1024 * 1024


def whole_block(shape):
    zeros = (0,) * len(shape)
    return pl.BlockSpec(shape, lambda *_: zeros, pipeline_mode=pl.Buffered(1))


def dot(a, b, a_dim, b_dim):
    return lax.dot_general(a, b, (((a_dim,), (b_dim,)), ((), ())), preferred_element_type=F32)


def split_pair(value):
    high = lax.reduce_precision(value, 8, 7)
    return jnp.concatenate([high, value - high], axis=-1).astype(BF)


def join_pair(pair, count):
    pair = pair.astype(F32)
    return pair[..., :count] + pair[..., count : 2 * count]


def forward_kernel(n_slice, n_expert, place, *refs):
    xs, dys = refs[:n_slice], refs[n_slice : 2 * n_slice]
    route_w, gate_a, up_a, down_a, gate_b, up_b, down_b = refs[2 * n_slice : 2 * n_slice + 7]
    grad_pre, weighted, route, acc = refs[2 * n_slice + 7 :]
    step = pl.program_id(0)
    units = gate_a.shape[1]

    for at in range(n_slice):

        @pl.when(step == at)
        def _(at=at):
            x, dy = xs[at][...], dys[at][...]
            for number, (source, weight, dim) in enumerate(
                (
                    (x, gate_a, 0),
                    (x, up_a, 0),
                    (dy, down_a, 1),
                    (x, gate_b, 0),
                    (x, up_b, 0),
                    (dy, down_b, 1),
                )
            ):
                part = dot(source, weight[...], 1, dim)
                if at == 0:
                    acc[number] = part
                else:
                    acc[number] += part

    @pl.when(step == n_slice - 1)
    def _():
        lane = lax.broadcasted_iota(jnp.int32, (route_w.shape[0], LANES), 1)
        own = place[1]
        total = jnp.zeros((route_w.shape[0], LANES), F32)
        for j in range(2):
            expert = jnp.bitwise_xor(own, j)
            gate_pre, up_pre, back = acc[3 * j], acc[3 * j + 1], acc[3 * j + 2]
            weight = jnp.sum(
                jnp.where(lane == expert, route_w[...].astype(F32), 0.0), axis=1, keepdims=True
            )
            logistic = jax.nn.sigmoid(gate_pre)
            active = gate_pre * logistic
            hidden = active * up_pre
            route_part = jnp.sum(back * hidden, axis=1, keepdims=True)
            high = route_part.astype(BF).astype(F32)
            total = total + jnp.where(lane == expert, high, 0.0)
            total = total + jnp.where(lane == expert + n_expert, route_part - high, 0.0)
            scaled = weight * back
            grad_pre[:, 2 * j * units : (2 * j + 1) * units] = (
                scaled * up_pre * logistic * (1.0 + gate_pre * (1.0 - logistic))
            ).astype(BF)
            grad_pre[:, (2 * j + 1) * units : (2 * j + 2) * units] = (scaled * active).astype(BF)
            weighted[:, j * units : (j + 1) * units] = (weight * hidden).astype(BF)
        route[...] = total.astype(BF)


def forward_values(place, xs, dys, route_w, mine, other, n_expert):
    n_slice = len(xs)
    rows, width = xs[0].shape
    units = mine[0].shape[1]
    wide = pl.BlockSpec((width, units), lambda s, p: (p[0] ^ s, 0))
    tall = pl.BlockSpec((units, width), lambda s, p: (0, p[0] ^ s))
    return pl.pallas_call(
        functools.partial(forward_kernel, n_slice, n_expert),
        grid_spec=pltpu.PrefetchScalarGridSpec(
            num_scalar_prefetch=1,
            grid=(n_slice,),
            in_specs=[whole_block((rows, width))] * (2 * n_slice)
            + [whole_block((rows, LANES))]
            + [wide, wide, tall] * 2,
            out_specs=[
                whole_block((rows, 4 * units)),
                whole_block((rows, 2 * units)),
                whole_block((rows, LANES)),
            ],
            scratch_shapes=[pltpu.VMEM((6, rows, units), F32)],
        ),
        out_shape=[
            jax.ShapeDtypeStruct((rows, 4 * units), BF),
            jax.ShapeDtypeStruct((rows, 2 * units), BF),
            jax.ShapeDtypeStruct((rows, LANES), BF),
        ],
        compiler_params=pltpu.CompilerParams(vmem_limit_bytes=VMEM_LIMIT),
        cost_estimate=pl.CostEstimate(
            flops=12 * rows * width * n_slice * units,
            bytes_accessed=2 * n_slice * width * (2 * rows + 6 * units),
            transcendentals=2 * rows * units,
        ),
        name="forward_values",
    )(place, *xs, *dys, route_w, *mine, *other)


def unit_kernel(lo, hi, tokens, with_route, place, grad_pre, *refs):
    if with_route:
        route, refs = refs[0], refs[1:]
    weights, outs = refs[:4], refs[4:]
    units = weights[0].shape[1]
    half = weights[0].shape[0] // 2
    grads = grad_pre[...]
    total = None
    for number, weight in enumerate(weights):
        part = dot(grads[:, number * units : (number + 1) * units], weight[...], 1, 1)
        total = part if total is None else total + part
    for m in range(lo):
        for h in range(hi):
            at = (h * lo + m) * tokens
            outs[m][h, :, :half] = total[at : at + tokens, :half].astype(outs[m].dtype)
            if with_route:
                outs[m][h, :, half:] = route[at : at + tokens, :].astype(outs[m].dtype)
    for h in range(hi):
        for m in range(lo):
            at = (h * lo + m) * tokens
            outs[lo + h][m] = total[at : at + tokens, half:].astype(outs[lo + h].dtype)


def unit_product(place, grad_pre, weights, slot, lo, hi, tokens, width, route=None):
    rows = grad_pre.shape[0]
    units = weights[0].shape[1]
    half = width // 2
    first = half + (LANES if route is not None else 0)
    wide = pl.BlockSpec((width, units), lambda i, p: (p[0] ^ slot, 0))
    shapes = [
        jax.ShapeDtypeStruct((hi, tokens, first), F32 if m == 0 else BF) for m in range(lo)
    ] + [jax.ShapeDtypeStruct((lo, tokens, half), F32 if h == 0 else BF) for h in range(hi)]
    extra = [] if route is None else [route]
    outs = pl.pallas_call(
        functools.partial(unit_kernel, lo, hi, tokens, route is not None),
        grid_spec=pltpu.PrefetchScalarGridSpec(
            num_scalar_prefetch=1,
            grid=(1,),
            in_specs=[whole_block(grad_pre.shape)]
            + [whole_block(r.shape) for r in extra]
            + [wide] * 4,
            out_specs=[whole_block(s.shape) for s in shapes],
        ),
        out_shape=shapes,
        compiler_params=pltpu.CompilerParams(vmem_limit_bytes=VMEM_LIMIT),
        cost_estimate=pl.CostEstimate(
            flops=8 * rows * width * units,
            bytes_accessed=8 * width * units + 2 * rows * (4 * units + 3 * width // 2),
            transcendentals=0,
        ),
        name="unit_product",
    )(place, grad_pre, *extra, *weights)
    return outs[:lo], outs[lo:]


def outer_kernel(n_slice, which, final, place, *refs):
    xs, dys = refs[:n_slice], refs[n_slice : 2 * n_slice]
    grad_pre, weighted = refs[2 * n_slice : 2 * n_slice + 2]
    rest = refs[2 * n_slice + 2 :]
    gate_out, up_out, down_out = rest[-3:]
    units = gate_out.shape[1]
    step = pl.program_id(0)
    for at in range(n_slice):

        @pl.when(step == at)
        def _(at=at):
            x, dy = xs[at][...], dys[at][...]
            both = dot(x, grad_pre[:, 2 * which * units : 2 * (which + 1) * units], 0, 0)
            gate, up = both[:, :units], both[:, units:]
            down = dot(weighted[:, which * units : (which + 1) * units], dy, 0, 0)
            if final:
                gate_in, up_in, down_in, down_w, fisher, anchor = rest[:6]
                gate = gate + gate_in[...].astype(F32)
                up = up + up_in[...].astype(F32)
                down = down + down_in[...].astype(F32)
                down = down + fisher[...] * (down_w[...].astype(F32) - anchor[...])
            gate_out[...] = gate.astype(BF)
            up_out[...] = up.astype(BF)
            down_out[...] = down.astype(BF)


def outer_products(place, xs, dys, grad_pre, weighted, which, final=()):
    n_slice = len(xs)
    rows, width = xs[0].shape
    units = grad_pre.shape[1] // 4
    wide = pl.BlockSpec((width, units), lambda s, p: (p[0] ^ s, 0))
    tall = pl.BlockSpec((units, width), lambda s, p: (0, p[0] ^ s))
    full = n_slice * width
    return pl.pallas_call(
        functools.partial(outer_kernel, n_slice, which, bool(final)),
        grid_spec=pltpu.PrefetchScalarGridSpec(
            num_scalar_prefetch=1,
            grid=(n_slice,),
            in_specs=[whole_block((rows, width))] * (2 * n_slice)
            + [whole_block(grad_pre.shape), whole_block(weighted.shape)]
            + ([wide, wide, tall, tall, tall, tall] if final else []),
            out_specs=[wide, wide, tall],
        ),
        out_shape=[
            jax.ShapeDtypeStruct((full, units), BF),
            jax.ShapeDtypeStruct((full, units), BF),
            jax.ShapeDtypeStruct((units, full), BF),
        ],
        compiler_params=pltpu.CompilerParams(vmem_limit_bytes=VMEM_LIMIT),
        cost_estimate=pl.CostEstimate(
            flops=6 * rows * full * units,
            bytes_accessed=full * (4 * rows + 6 * units + (16 * units if final else 0)),
            transcendentals=0,
        ),
        name="outer_final" if final else "outer_other",
    )(place, *xs, *dys, grad_pre, weighted, *final)


def per_device(
    n_expert,
    n_slice,
    tokens,
    cotangent,
    route_ids,
    route_weights,
    gate_weight,
    up_weight,
    down_weight,
    fisher,
    anchor,
):
    count, width = tokens.shape
    chips = n_expert // 2
    lo = 1 << ((chips.bit_length() - 1) // 2)
    hi = chips // lo
    own_e, own_f = lax.axis_index("expert"), lax.axis_index("ffn")
    place = jnp.stack([own_f, own_e]).astype(jnp.int32)

    def over_expert(value, mask):
        pairs = [(i, i ^ mask) for i in range(n_expert)]
        return lax.ppermute(value, "expert", pairs)

    def over_lo(value, mask):
        return over_expert(value, 2 * mask)

    def over_hi(value, mask):
        return over_expert(value, 2 * lo * mask)

    def over_slice(value, mask):
        return lax.ppermute(value, "ffn", [(i, i ^ mask) for i in range(n_slice)])

    def collect(value, send, number, axis):
        return jnp.stack([value] + [send(value, m) for m in range(1, number)], axis=axis)

    named = route_ids[:, :, None] == jnp.arange(LANES, dtype=jnp.int32)[None, None, :]
    route_row = jnp.sum(
        jnp.where(named, route_weights.astype(F32)[:, :, None], 0.0), axis=1
    ).astype(BF)

    x_parts = [tokens] + [over_slice(tokens, s) for s in range(1, n_slice)]
    dy_parts = [cotangent] + [over_slice(cotangent, s) for s in range(1, n_slice)]
    dy_parts[0] = jnp.concatenate([cotangent, route_row], axis=1)
    xs, dys = [], []
    for s in range(n_slice):
        x = collect(collect(x_parts[s], over_lo, lo, 0), over_hi, hi, 0)
        dy = collect(collect(dy_parts[s], over_hi, hi, 0), over_lo, lo, 1)
        xs.append(x.reshape(chips * count, -1))
        dys.append(dy.reshape(chips * count, -1))
    route_w = dys[0][:, width:]
    dys[0] = dys[0][:, :width]

    mine = (gate_weight[0], up_weight[0], down_weight[0])
    other = tuple(over_expert(w, 1) for w in mine)
    grad_pre, weighted, route = forward_values(place, xs, dys, route_w, mine, other, n_expert)

    projections = (mine[0], mine[1], other[0], other[1])
    half = width // 2
    shares, route_sum = {}, None
    for s in reversed(range(n_slice)):
        first = s == n_slice - 1
        a, b = unit_product(
            place, grad_pre, projections, s, lo, hi, count, width, route if first else None
        )
        a_sum = a[0] + sum(over_lo(a[m], m).astype(F32) for m in range(1, lo))
        b_sum = b[0] + sum(over_hi(b[h], h).astype(F32) for h in range(1, hi))
        if first:
            pair = split_pair(join_pair(a_sum[..., half:], n_expert))
            pad = jnp.zeros(pair.shape[:-1] + (LANES - 2 * n_expert,), BF)
            a_out = jnp.concatenate([a_sum[..., :half].astype(BF), pair, pad], axis=-1)
        else:
            a_out = a_sum.astype(BF)
        a_own = a_sum[0] + sum(over_hi(a_out[h], h).astype(F32) for h in range(1, hi))
        b_out = b_sum.astype(BF)
        b_own = b_sum[0] + sum(over_lo(b_out[m], m).astype(F32) for m in range(1, lo))
        if first:
            route_sum = join_pair(a_own[:, half:], n_expert)
            a_own = a_own[:, :half]
        shares[s] = jnp.concatenate([a_own, b_own], axis=1)
    pair = split_pair(route_sum)
    pad = jnp.zeros((count, LANES - 2 * n_expert), BF)
    total, route_total = shares[0], route_sum
    for s in range(1, n_slice):
        got = over_slice(jnp.concatenate([shares[s].astype(BF), pair, pad], axis=1), s)
        total = total + got[:, :width].astype(F32)
        route_total = route_total + join_pair(got[:, width:], n_expert)
    grad_tokens = total.astype(BF)
    chosen = route_ids[:, :, None] == jnp.arange(n_expert, dtype=jnp.int32)[None, None, :]
    grad_route = jnp.sum(jnp.where(chosen, route_total[:, None, :], 0.0), axis=2)

    sent = outer_products(place, xs, dys, grad_pre, weighted, 1)
    got = [over_expert(g, 1) for g in sent]
    grads = outer_products(
        place, xs, dys, grad_pre, weighted, 0, (*got, mine[2], fisher[0], anchor[0])
    )
    return (grad_tokens, grad_route, grads[0][None], grads[1][None], grads[2][None])


def solution(mesh):
    return jax.shard_map(
        functools.partial(per_device, mesh.shape["expert"], mesh.shape["ffn"]),
        mesh=mesh,
        in_specs=(
            P("expert", "ffn"),
            P("expert", "ffn"),
            P("expert", None),
            P("expert", None),
            P("expert", None, "ffn"),
            P("expert", None, "ffn"),
            P("expert", "ffn", None),
            P("expert", "ffn", None),
            P("expert", "ffn", None),
        ),
        out_specs=(
            P("expert", "ffn"),
            P("expert", None),
            P("expert", None, "ffn"),
            P("expert", None, "ffn"),
            P("expert", "ffn", None),
        ),
        check_vma=False,
    )
```

```python
import functools
import math

import jax
import jax.numpy as jnp
from jax import lax
from jax.experimental import pallas as pl
from jax.experimental.pallas import tpu as pltpu
from jax.sharding import PartitionSpec as P

BF = jnp.bfloat16
F32 = jnp.float32
LANES = 128
MIB = 1024 * 1024


def whole_block(shape):
    zeros = (0,) * len(shape)
    return pl.BlockSpec(shape, lambda *_: zeros, pipeline_mode=pl.Buffered(1))


def dot(a, b, a_dim, b_dim):
    return lax.dot_general(a, b, (((a_dim,), (b_dim,)), ((), ())), preferred_element_type=F32)


def after(value, *first):
    return lax.optimization_barrier((value, *first))[0]


def params(need):
    return pltpu.CompilerParams(vmem_limit_bytes=min(need + 12 * MIB, 58 * MIB))


def add_slice(x, dy, weights, before):
    values = []
    for number, weight in enumerate(weights):
        from_dy = number % 3 == 2
        part = dot(dy if from_dy else x, weight[...], 1, 1 if from_dy else 0)
        values.append(part if before is None else part + before[number])
    return values


def forward_kernel(first, place, x_ref, dy_ref, *refs):
    weights, refs = refs[:6], refs[6:]
    values = add_slice(x_ref[...], dy_ref[...], weights, None if first else refs[0])
    for number in range(6):
        refs[-1][number] = values[number]


def rest_kernel(n_expert, slots, place, *refs):
    sources, refs = refs[: 2 * slots], refs[2 * slots :]
    weights, before, route_w = refs[:6], refs[6], refs[7]
    mine, other, route, held = refs[8:]
    units = weights[0].shape[1]
    step = pl.program_id(0)

    for at in range(slots - 1):

        @pl.when(step == at)
        def _(at=at):
            x, dy = sources[2 * at][...], sources[2 * at + 1][...]
            values = add_slice(x, dy, weights, held if at else before)
            for number in range(6):
                held[number] = values[number]

    @pl.when(step == slots - 1)
    def _():
        values = add_slice(sources[-2][...], sources[-1][...], weights, held)
        lane = lax.broadcasted_iota(jnp.int32, route.shape, 1)
        total = jnp.zeros(route.shape, F32)
        for j, acts in enumerate((mine, other)):
            expert = jnp.bitwise_xor(place[1], j)
            gate_pre, up_pre, back = values[3 * j : 3 * j + 3]
            weight = jnp.sum(
                jnp.where(lane == expert, route_w[...].astype(F32), 0.0), axis=1, keepdims=True
            )
            logistic = jax.nn.sigmoid(gate_pre)
            active = gate_pre * logistic
            hidden = active * up_pre
            route_part = jnp.sum(back * hidden, axis=1, keepdims=True)
            high = route_part.astype(BF).astype(F32)
            total = total + jnp.where(lane == expert, high, 0.0)
            total = total + jnp.where(lane == expert + n_expert, route_part - high, 0.0)
            scaled = weight * back
            acts[:, :units] = (
                scaled * up_pre * logistic * (1.0 + gate_pre * (1.0 - logistic))
            ).astype(BF)
            acts[:, units : 2 * units] = (scaled * active).astype(BF)
            acts[:, 2 * units :] = (weight * hidden).astype(BF)
        route[...] = total.astype(BF)


def column_block(rows, width, column):
    return pl.BlockSpec(
        (rows, width), lambda i, p: (0, column), pipeline_mode=pl.Buffered(1)
    )


def forward_cost(rows, width, units, slots):
    return pl.CostEstimate(
        flops=12 * rows * width * units * slots,
        bytes_accessed=2 * width * (2 * rows + 6 * units) * slots + 24 * rows * units,
        transcendentals=2 * rows * units,
    )


def forward_slice(place, slot, pair, weights, before, width):
    rows = pair.shape[0]
    units = weights[0].shape[1]
    wide = pl.BlockSpec((width, units), lambda i, p: (p[0] ^ slot, 0))
    tall = pl.BlockSpec((units, width), lambda i, p: (0, p[0] ^ slot))
    specs = [column_block(rows, width, column) for column in range(2)] + [wide, wide, tall] * 2
    extra = [] if before is None else [before]
    return pl.pallas_call(
        functools.partial(forward_kernel, before is None),
        grid_spec=pltpu.PrefetchScalarGridSpec(
            num_scalar_prefetch=1,
            grid=(1,),
            in_specs=specs + [whole_block(e.shape) for e in extra],
            out_specs=whole_block((6, rows, units)),
        ),
        out_shape=jax.ShapeDtypeStruct((6, rows, units), F32),
        compiler_params=params(58 * MIB),
        cost_estimate=forward_cost(rows, width, units, 1),
        name="forward_slice",
    )(place, pair, pair, *weights, *extra)


def forward_rest(place, pairs, weights, before, route_w, n_expert, width, done):
    rows = pairs[0].shape[0]
    units = weights[0].shape[1]
    slots = len(pairs)
    wide = pl.BlockSpec((width, units), lambda i, p: (p[0] ^ (i + done), 0))
    tall = pl.BlockSpec((units, width), lambda i, p: (0, p[0] ^ (i + done)))
    return pl.pallas_call(
        functools.partial(rest_kernel, n_expert, slots),
        grid_spec=pltpu.PrefetchScalarGridSpec(
            num_scalar_prefetch=1,
            grid=(slots,),
            in_specs=[column_block(rows, width, column) for column in range(2)] * slots
            + [wide, wide, tall] * 2
            + [whole_block(before.shape), column_block(rows, LANES, 2 * width // LANES)],
            out_specs=[
                whole_block((rows, 3 * units)),
                whole_block((rows, 3 * units)),
                whole_block((rows, LANES)),
            ],
            scratch_shapes=[pltpu.VMEM((6, rows, units), F32)],
        ),
        out_shape=[
            jax.ShapeDtypeStruct((rows, 3 * units), BF),
            jax.ShapeDtypeStruct((rows, 3 * units), BF),
            jax.ShapeDtypeStruct((rows, LANES), BF),
        ],
        compiler_params=params(
            4 * rows * width * slots + 24 * width * units + 120 * rows * units
        ),
        cost_estimate=forward_cost(rows, width, units, slots),
        name="forward_rest",
    )(place, *[p for pair in pairs for p in (pair, pair)], *weights, before, route_w)


def unit_kernel(tokens, with_route, place, mine, other, *refs):
    if with_route:
        route, refs = refs[0], refs[1:]
    weights, outs = refs[:4], refs[4:]
    width, units = weights[0].shape
    total = None
    for number, weight in enumerate(weights):
        acts = mine if number < 2 else other
        at = (number % 2) * units
        part = dot(acts[:, at : at + units], weight[...], 1, 1)
        total = part if total is None else total + part
    for block, out in enumerate(outs):
        at = block * tokens
        out[:, :width] = total[at : at + tokens].astype(out.dtype)
        if with_route:
            out[:, width:] = route[at : at + tokens, :].astype(out.dtype)


def unit_product(place, mine, other, weights, slot, tokens, width, route=None):
    rows = mine.shape[0]
    units = weights[0].shape[1]
    wide = pl.BlockSpec((width, units), lambda i, p: (p[0] ^ slot, 0))
    acts = column_block(rows, 2 * units, 0)
    columns = width + (0 if route is None else LANES)
    shapes = [
        jax.ShapeDtypeStruct((tokens, columns), F32 if block == 0 else BF)
        for block in range(rows // tokens)
    ]
    extra = [] if route is None else [route]
    return pl.pallas_call(
        functools.partial(unit_kernel, tokens, route is not None),
        grid_spec=pltpu.PrefetchScalarGridSpec(
            num_scalar_prefetch=1,
            grid=(1,),
            in_specs=[acts, acts] + [whole_block(r.shape) for r in extra] + [wide] * 4,
            out_specs=[whole_block(s.shape) for s in shapes],
        ),
        out_shape=shapes,
        compiler_params=params(16 * width * units + 16 * rows * units + 12 * rows * width),
        cost_estimate=pl.CostEstimate(
            flops=8 * rows * width * units,
            bytes_accessed=8 * width * units + 2 * rows * (4 * units + 3 * width // 2),
            transcendentals=0,
        ),
        name="unit_product",
    )(place, mine, other, *extra, *weights)


def outer_kernel(pieces, rows, down, place, acts, got, *refs):
    n_slice = len(pieces) // 2
    sources, refs = refs[: 2 * n_slice], refs[2 * n_slice :]
    if down:
        down_w, fisher, anchor, out = refs[:4]
    else:
        gate_out, up_out = refs[:2]
    held, grads, sems = refs[-3:]
    width = held.shape[2]
    units = acts.shape[1] // 3
    step = pl.program_id(0)

    def copies(slot):
        return [
            pltpu.make_async_copy(
                sources[side * n_slice + slot].at[
                    :, pl.ds(pieces[side * n_slice + slot] * width, width)
                ],
                held.at[slot, pl.ds(side * rows, rows)],
                sems.at[slot, side],
            )
            for side in range(2)
        ]

    @pl.when(step == 0)
    def _():
        for slot in range(n_slice):
            for copy in copies(slot):
                copy.start()
        grads[:rows] = acts[...]
        grads[rows:] = got[...]

    for slot in range(n_slice):

        @pl.when(step == slot)
        def _(slot=slot):
            for copy in copies(slot):
                copy.wait()

    block = held[step]
    if down:
        value = dot(grads[:, 2 * units :], block, 0, 0)
        value = value + fisher[...] * (down_w[...].astype(F32) - anchor[...])
        out[...] = value.astype(BF)
    else:
        value = dot(block, grads[:, : 2 * units], 0, 0)
        gate_out[...] = value[:, :units].astype(BF)
        up_out[...] = value[:, units:].astype(BF)


def outer_products(place, pieces, acts, got, width, penalty=()):
    n_slice = len(pieces) // 2
    rows = acts.shape[0]
    units = acts.shape[1] // 3
    full = n_slice * width
    down = bool(penalty)
    wide = pl.BlockSpec((width, units), lambda s, p: (p[0] ^ s, 0))
    tall = pl.BlockSpec((units, width), lambda s, p: (0, p[0] ^ s))
    anywhere = pl.BlockSpec(memory_space=pl.ANY)
    return pl.pallas_call(
        functools.partial(outer_kernel, tuple(p[1] for p in pieces), rows, down),
        grid_spec=pltpu.PrefetchScalarGridSpec(
            num_scalar_prefetch=1,
            grid=(n_slice,),
            in_specs=[whole_block(acts.shape), whole_block(got.shape)]
            + [anywhere] * (2 * n_slice)
            + [tall] * len(penalty),
            out_specs=[tall] if down else [wide, wide],
            scratch_shapes=[
                pltpu.VMEM((n_slice, 2 * rows, width), BF),
                pltpu.VMEM((2 * rows, 3 * units), BF),
                pltpu.SemaphoreType.DMA((n_slice, 2)),
            ],
        ),
        out_shape=[jax.ShapeDtypeStruct((units, full), BF)]
        if down
        else [jax.ShapeDtypeStruct((full, units), BF)] * 2,
        compiler_params=params(58 * MIB),
        cost_estimate=pl.CostEstimate(
            flops=4 * rows * full * units * (1 if down else 2),
            bytes_accessed=full * (4 * rows + units * (12 if down else 4)),
            transcendentals=0,
        ),
        name="outer_down" if down else "outer_gate_up",
    )(place, acts, got, *[p[0] for p in pieces], *penalty)


def repack(tail, count):
    lane = lax.broadcasted_iota(jnp.int32, tail.shape, 1)
    value = tail + pltpu.roll(tail, LANES - count, 1)
    high = value.astype(BF).astype(F32)
    low = pltpu.roll(value - high, count, 1)
    return jnp.where(lane < count, high, jnp.where(lane < 2 * count, low, 0.0))


def call_small(kernel, name, shapes, *args):
    size = sum(4 * math.prod(a.shape) for a in args) + sum(4 * math.prod(s.shape) for s in shapes)
    return pl.pallas_call(
        kernel,
        grid=(1,),
        in_specs=[whole_block(a.shape) for a in args],
        out_specs=[whole_block(s.shape) for s in shapes],
        out_shape=shapes,
        compiler_params=params(2 * size),
        cost_estimate=pl.CostEstimate(flops=size, bytes_accessed=size, transcendentals=0),
        name=name,
    )(*args)


def slice_sum_kernel(n_got, n_expert, width, own, *refs):
    gots, rest = refs[:n_got], refs[n_got:]
    value = own[...]
    for got in gots:
        value = value + got[...].astype(F32)
    if value.shape[1] > width:
        send, pair_out = rest
        pair = repack(value[:, width:], n_expert).astype(BF)
        pair_out[...] = pair
    else:
        pair_in, send = rest
        pair = pair_in[...]
    send[:, :width] = value[:, :width].astype(BF)
    send[:, width:] = pair


def slice_sum(own, gots, pair, n_expert, width):
    tokens = own.shape[0]
    shapes = [jax.ShapeDtypeStruct((tokens, width + LANES), BF)]
    if pair is None:
        shapes.append(jax.ShapeDtypeStruct((tokens, LANES), BF))
    kernel = functools.partial(slice_sum_kernel, len(gots), n_expert, width)
    extra = [] if pair is None else [pair]
    out = call_small(kernel, "slice_sum", shapes, own, *gots, *extra)
    return out[0], (out[1] if pair is None else pair)


def final_sum_kernel(n_got, n_far, n_expert, own, pair, ids, *refs):
    gots, fars, (grad, route) = refs[:n_got], refs[n_got : n_got + n_far], refs[n_got + n_far :]
    width = own.shape[1]
    value, tail = own[...], pair[...].astype(F32)
    for got in gots:
        value = value + got[...].astype(F32)
    for far in fars:
        value = value + far[:, :width].astype(F32)
        tail = tail + far[:, width:].astype(F32)
    grad[...] = value.astype(BF)
    tail = tail + pltpu.roll(tail, LANES - n_expert, 1)
    lane = lax.broadcasted_iota(jnp.int32, tail.shape, 1)
    for k in range(route.shape[1]):
        chosen = jnp.logical_and(lane == ids[:, k : k + 1], lane < n_expert)
        route[:, k : k + 1] = jnp.sum(jnp.where(chosen, tail, 0.0), axis=1, keepdims=True)


def final_sum(own, gots, fars, pair, ids, n_expert):
    shapes = [jax.ShapeDtypeStruct(own.shape, BF), jax.ShapeDtypeStruct(ids.shape, F32)]
    kernel = functools.partial(final_sum_kernel, len(gots), len(fars), n_expert)
    return call_small(kernel, "final_sum", shapes, own, pair, ids, *gots, *fars)


def per_device(
    n_expert,
    n_slice,
    tokens,
    cotangent,
    route_ids,
    route_weights,
    gate_weight,
    up_weight,
    down_weight,
    fisher,
    anchor,
):
    count, width = tokens.shape
    chips = n_expert // 2
    rows = chips * count
    lo = 1 << ((chips.bit_length() - 1) // 2)
    hi = chips // lo
    own_e, own_f = lax.axis_index("expert"), lax.axis_index("ffn")
    place = jnp.stack([own_f, own_e]).astype(jnp.int32)

    def over_expert(value, mask):
        return lax.ppermute(value, "expert", [(i, i ^ mask) for i in range(n_expert)])

    def over_lo(value, mask):
        return over_expert(value, 2 * mask)

    def over_hi(value, mask):
        return over_expert(value, 2 * lo * mask)

    def over_slice(value, mask):
        return lax.ppermute(value, "ffn", [(i, i ^ mask) for i in range(n_slice)])

    def collect(value, send, number, axis):
        return jnp.stack([value] + [send(value, m) for m in range(1, number)], axis=axis)

    named = route_ids[:, :, None] == jnp.arange(LANES, dtype=jnp.int32)[None, None, :]
    route_row = jnp.sum(
        jnp.where(named, route_weights.astype(F32)[:, :, None], 0.0), axis=1
    ).astype(BF)

    both = jnp.concatenate([tokens, cotangent], axis=1)
    parts = [both] + [over_slice(both, s) for s in range(1, n_slice)]
    parts[1] = jnp.concatenate([parts[1], route_row], axis=1)
    hops = [[both] + [over_expert(both, 2 * m) for m in range(1, chips)]]
    part = after(parts[1], *hops[0][1:])
    hops.append([part] + [over_expert(part, 2 * m) for m in range(1, chips)])
    mine = (gate_weight[0], up_weight[0], down_weight[0])
    weights = mine + tuple(over_expert(after(w, parts[2]), 1) for w in mine)
    rest = []
    for s in range(2, n_slice):
        value = after(parts[s], *hops[1][1:])
        rest.append(collect(value, over_lo, lo, 0) if s % 2 == 0 else collect(value, over_hi, hi, 0))
    near = [jnp.stack(h).reshape(rows, -1) for h in hops]
    acc = forward_slice(place, 0, near[0], weights, None, width)
    acc = forward_slice(place, 1, near[1], weights, acc, width)
    got_near = tuple(over_expert(v, 1) for v in near)
    for at, value in enumerate(rest):
        send, number, axis = (over_hi, hi, 0) if at % 2 == 0 else (over_lo, lo, 1)
        got = [send(value, m) for m in range(1, number)]
        value = after(value, acc, *got_near)
        rest[at] = jnp.stack([value] + got, axis=axis).reshape(rows, -1)
    acts, acts_other, route = forward_rest(
        place, rest, weights, acc, near[1], n_expert, width, 2
    )

    got_acts = over_expert(acts_other, 1)
    got_rest = tuple(over_expert(v, 1) for v in rest)
    pieces = [
        [(v, which) for v in (*near, *rest, *got_near, *got_rest)] for which in range(2)
    ]
    ready = after(place, *got_rest)

    projections = (weights[0], weights[1], weights[3], weights[4])
    order = list(reversed(range(n_slice)))
    parts, fars, pair, late = [], [], None, ready
    for at, s in enumerate(order):
        if at == 1:
            late = after(late, got_acts)
        outs = unit_product(
            late, acts, acts_other, projections, s, count, width, route if at == 0 else None
        )
        parts.append(
            (outs[0], [over_expert(v, 2 * (block + 1)) for block, v in enumerate(outs[1:])])
        )
        if at == n_slice - 2:
            send, pair = slice_sum(*parts[0], None, n_expert, width)
            fars.append(over_slice(send, order[0]))
            late = after(late, send)
    for at, s in enumerate(order[:-1]):
        if at > 0:
            own, got = parts[at]
            if at > 1 and at == n_slice - 2:
                own = after(own, grad_gate)
            send, pair = slice_sum(own, got, pair, n_expert, width)
            fars.append(over_slice(send, s))
        if at == n_slice - 3:
            late = after(place, send)
            grad_gate, grad_up = outer_products(late, pieces[0], acts, got_acts, width)
    late = after(place, send, grad_gate)
    (grad_down,) = outer_products(
        late, pieces[1], acts, got_acts, width, (mine[2], fisher[0], anchor[0])
    )
    own = after(parts[-1][0], grad_down)
    grad_tokens, grad_route = final_sum(own, parts[-1][1], fars, pair, route_ids, n_expert)
    return (grad_tokens, grad_route, grad_gate[None], grad_up[None], grad_down[None])


def solution(mesh):
    return jax.shard_map(
        functools.partial(per_device, mesh.shape["expert"], mesh.shape["ffn"]),
        mesh=mesh,
        in_specs=(
            P("expert", "ffn"),
            P("expert", "ffn"),
            P("expert", None),
            P("expert", None),
            P("expert", None, "ffn"),
            P("expert", None, "ffn"),
            P("expert", "ffn", None),
            P("expert", "ffn", None),
            P("expert", "ffn", None),
        ),
        out_specs=(
            P("expert", "ffn"),
            P("expert", None),
            P("expert", None, "ffn"),
            P("expert", None, "ffn"),
            P("expert", "ffn", None),
        ),
        check_vma=False,
    )
```

```python
import functools
import math

import jax
import jax.numpy as jnp
from jax import lax
from jax.experimental import pallas as pl
from jax.experimental.pallas import tpu as pltpu
from jax.sharding import PartitionSpec as P

BF = jnp.bfloat16
F32 = jnp.float32
LANES = 128
MIB = 1024 * 1024


def whole_block(shape):
    zeros = (0,) * len(shape)
    return pl.BlockSpec(shape, lambda *_: zeros, pipeline_mode=pl.Buffered(1))


def dot(a, b, a_dim, b_dim):
    return lax.dot_general(a, b, (((a_dim,), (b_dim,)), ((), ())), preferred_element_type=F32)


def after(value, *first):
    return lax.optimization_barrier((value, *first))[0]


def params(need):
    return pltpu.CompilerParams(vmem_limit_bytes=min(need + 12 * MIB, 58 * MIB))


def add_slice(x, dy, weights, before):
    values = []
    for number, weight in enumerate(weights):
        from_dy = number % 3 == 2
        part = dot(dy if from_dy else x, weight[...], 1, 1 if from_dy else 0)
        values.append(part if before is None else part + before[number])
    return values


def near_kernel(own_ref, near_ref, weights, out):
    width = weights[0].shape[0]
    step = pl.program_id(0)
    for at, (ref, base) in enumerate(((own_ref, 0), (near_ref, 0), (near_ref, 2))):

        @pl.when(step == at)
        def _(at=at, ref=ref, base=base):
            x = ref[:, base * width : (base + 1) * width]
            dy = ref[:, (base + 1) * width : (base + 2) * width]
            values = add_slice(x, dy, weights, out if at else None)
            for number in range(6):
                out[number] = values[number]


def forward_kernel(place, own_ref, near_ref, *refs):
    near_kernel(own_ref, near_ref, refs[:6], refs[6])


def rest_kernel(n_expert, slots, place, *refs):
    sources, refs = refs[: 2 * slots], refs[2 * slots :]
    weights, before, route_w = refs[:6], refs[6], refs[7]
    mine, other, route, held = refs[8:]
    units = weights[0].shape[1]
    step = pl.program_id(0)

    for at in range(slots - 1):

        @pl.when(step == at)
        def _(at=at):
            x, dy = sources[2 * at][...], sources[2 * at + 1][...]
            values = add_slice(x, dy, weights, held if at else before)
            for number in range(6):
                held[number] = values[number]

    @pl.when(step == slots - 1)
    def _():
        values = add_slice(
            sources[-2][...], sources[-1][...], weights, held if slots > 1 else before
        )
        lane = lax.broadcasted_iota(jnp.int32, route.shape, 1)
        total = jnp.zeros(route.shape, F32)
        for j, acts in enumerate((mine, other)):
            expert = jnp.bitwise_xor(place[1], j)
            gate_pre, up_pre, back = values[3 * j : 3 * j + 3]
            weight = jnp.sum(
                jnp.where(lane == expert, route_w[...].astype(F32), 0.0), axis=1, keepdims=True
            )
            logistic = jax.nn.sigmoid(gate_pre)
            active = gate_pre * logistic
            hidden = active * up_pre
            route_part = jnp.sum(back * hidden, axis=1, keepdims=True)
            high = route_part.astype(BF).astype(F32)
            total = total + jnp.where(lane == expert, high, 0.0)
            total = total + jnp.where(lane == expert + n_expert, route_part - high, 0.0)
            scaled = weight * back
            acts[:, :units] = (
                scaled * up_pre * logistic * (1.0 + gate_pre * (1.0 - logistic))
            ).astype(BF)
            acts[:, units : 2 * units] = (scaled * active).astype(BF)
            acts[:, 2 * units :] = (weight * hidden).astype(BF)
        route[...] = total.astype(BF)


def column_block(rows, width, column):
    return pl.BlockSpec(
        (rows, width), lambda i, p: (0, column), pipeline_mode=pl.Buffered(1)
    )


def forward_cost(rows, width, units, slots):
    return pl.CostEstimate(
        flops=12 * rows * width * units * slots,
        bytes_accessed=2 * width * (2 * rows + 6 * units) * slots + 24 * rows * units,
        transcendentals=2 * rows * units,
    )


def forward_near(place, own, near, weights, width):
    rows = own.shape[0]
    units = weights[0].shape[1]
    wide = pl.BlockSpec((width, units), lambda i, p: (p[0] ^ i, 0))
    tall = pl.BlockSpec((units, width), lambda i, p: (0, p[0] ^ i))
    return pl.pallas_call(
        forward_kernel,
        grid_spec=pltpu.PrefetchScalarGridSpec(
            num_scalar_prefetch=1,
            grid=(3,),
            in_specs=[whole_block(own.shape), whole_block(near.shape)]
            + [wide, wide, tall] * 2,
            out_specs=whole_block((6, rows, units)),
        ),
        out_shape=jax.ShapeDtypeStruct((6, rows, units), F32),
        compiler_params=params(14 * MIB),
        cost_estimate=forward_cost(rows, width, units, 3),
        name="forward_near",
    )(place, own, near, *weights)


def forward_rest(place, pairs, weights, before, route_w, n_expert, width, done):
    rows = pairs[0].shape[0]
    units = weights[0].shape[1]
    slots = len(pairs)
    wide = pl.BlockSpec((width, units), lambda i, p: (p[0] ^ (i + done), 0))
    tall = pl.BlockSpec((units, width), lambda i, p: (0, p[0] ^ (i + done)))
    return pl.pallas_call(
        functools.partial(rest_kernel, n_expert, slots),
        grid_spec=pltpu.PrefetchScalarGridSpec(
            num_scalar_prefetch=1,
            grid=(slots,),
            in_specs=[column_block(rows, width, column) for column in range(2)] * slots
            + [wide, wide, tall] * 2
            + [whole_block(before.shape), column_block(rows, LANES, 4 * width // LANES)],
            out_specs=[
                whole_block((rows, 3 * units)),
                whole_block((rows, 3 * units)),
                whole_block((rows, LANES)),
            ],
            scratch_shapes=[pltpu.VMEM((6, rows, units), F32)],
        ),
        out_shape=[
            jax.ShapeDtypeStruct((rows, 3 * units), BF),
            jax.ShapeDtypeStruct((rows, 3 * units), BF),
            jax.ShapeDtypeStruct((rows, LANES), BF),
        ],
        compiler_params=params(
            4 * rows * width * slots + 24 * width * units + 120 * rows * units
        ),
        cost_estimate=forward_cost(rows, width, units, slots),
        name="forward_rest",
    )(place, *[p for pair in pairs for p in (pair, pair)], *weights, before, route_w)


def unit_kernel(tokens, slots, with_route, place, mine, other, *refs):
    if with_route:
        route, refs = refs[0], refs[1:]
    weights, outs = refs[:4], refs[4:]
    width, units = weights[0].shape
    step = pl.program_id(0)
    total = None
    for number, weight in enumerate(weights):
        acts = mine if number < 2 else other
        at = (number % 2) * units
        part = dot(acts[:, at : at + units], weight[...], 1, 1)
        total = part if total is None else total + part
    for slot in range(slots):

        @pl.when(step == slot)
        def _(slot=slot):
            for block, out in enumerate(outs):
                rows = pl.ds(block * tokens, tokens)
                value = total[block * tokens : (block + 1) * tokens]
                out[:, slot * width : (slot + 1) * width] = value.astype(out.dtype)
                if with_route and slot == 0:
                    out[:, slots * width :] = route[rows, :].astype(out.dtype)


def unit_product(place, mine, other, weights, group, tokens, width, route=None):
    rows = mine.shape[0]
    units = weights[0].shape[1]
    slots, top = len(group), group[0]
    wide = pl.BlockSpec((width, units), lambda i, p: (p[0] ^ (top - i), 0))
    acts = column_block(rows, 2 * units, 0)
    columns = slots * width + (0 if route is None else LANES)
    shapes = [
        jax.ShapeDtypeStruct((tokens, columns), F32 if block == 0 else BF)
        for block in range(rows // tokens)
    ]
    extra = [] if route is None else [route]
    return pl.pallas_call(
        functools.partial(unit_kernel, tokens, slots, route is not None),
        grid_spec=pltpu.PrefetchScalarGridSpec(
            num_scalar_prefetch=1,
            grid=(slots,),
            in_specs=[acts, acts] + [whole_block(r.shape) for r in extra] + [wide] * 4,
            out_specs=[whole_block(s.shape) for s in shapes],
        ),
        out_shape=shapes,
        compiler_params=params(
            16 * width * units + 16 * rows * units + (8 + 4 * slots) * rows * width
        ),
        cost_estimate=pl.CostEstimate(
            flops=8 * rows * width * units * slots,
            bytes_accessed=8 * width * units * slots + 3 * rows * width * slots,
            transcendentals=0,
        ),
        name="unit_product",
    )(place, mine, other, *extra, *weights)


def outer_kernel(pieces, n_source, rows, down, place, acts, got, *refs):
    n_slice = len(pieces)
    sources, refs = refs[:n_source], refs[n_source:]
    if down:
        penalty, out = refs[:2]
    else:
        gate_out, up_out = refs[:2]
    held, grads, sems = refs[-3:]
    width = held.shape[2]
    units = acts.shape[1] // 3
    step = pl.program_id(0)

    def copies(slot):
        out = []
        for number, (source, index, column, at) in enumerate(pieces[slot]):
            ref = sources[source]
            ref = ref if index is None else ref.at[index]
            out.append(
                pltpu.make_async_copy(
                    ref.at[:, pl.ds(column * width, width)],
                    held.at[slot, pl.ds(at, ref.shape[0])],
                    sems.at[slot, number],
                )
            )
        return out

    @pl.when(step == 0)
    def _():
        for slot in range(n_slice):
            for copy in copies(slot):
                copy.start()
        grads[:rows] = acts[...]
        grads[rows:] = got[...]

    for slot in range(n_slice):

        @pl.when(step == slot)
        def _(slot=slot):
            for copy in copies(slot):
                copy.wait()

    block = held[step]
    if down:
        value = dot(grads[:, 2 * units :], block, 0, 0)
        out[...] = (value + penalty[...]).astype(BF)
    else:
        value = dot(block, grads[:, : 2 * units], 0, 0)
        gate_out[...] = value[:, :units].astype(BF)
        up_out[...] = value[:, units:].astype(BF)


def outer_products(place, sources, pieces, acts, got, width, penalty=None):
    n_slice = len(pieces)
    rows = acts.shape[0]
    units = acts.shape[1] // 3
    full = n_slice * width
    down = penalty is not None
    wide = pl.BlockSpec((width, units), lambda s, p: (p[0] ^ s, 0))
    tall = pl.BlockSpec((units, width), lambda s, p: (0, p[0] ^ s))
    anywhere = pl.BlockSpec(memory_space=pl.ANY)
    return pl.pallas_call(
        functools.partial(outer_kernel, pieces, len(sources), rows, down),
        grid_spec=pltpu.PrefetchScalarGridSpec(
            num_scalar_prefetch=1,
            grid=(n_slice,),
            in_specs=[whole_block(acts.shape), whole_block(got.shape)]
            + [anywhere] * len(sources)
            + [tall] * down,
            out_specs=[tall] if down else [wide, wide],
            scratch_shapes=[
                pltpu.VMEM((n_slice, 2 * rows, width), BF),
                pltpu.VMEM((2 * rows, 3 * units), BF),
                pltpu.SemaphoreType.DMA((n_slice, max(len(p) for p in pieces))),
            ],
        ),
        out_shape=[jax.ShapeDtypeStruct((units, full), BF)]
        if down
        else [jax.ShapeDtypeStruct((full, units), BF)] * 2,
        compiler_params=params(58 * MIB),
        cost_estimate=pl.CostEstimate(
            flops=4 * rows * full * units * (1 if down else 2),
            bytes_accessed=full * (4 * rows + units * (6 if down else 4)),
            transcendentals=0,
        ),
        name="outer_down" if down else "outer_gate_up",
    )(place, acts, got, *sources, *([penalty] if down else []))


def repack(tail, count):
    lane = lax.broadcasted_iota(jnp.int32, tail.shape, 1)
    value = tail + pltpu.roll(tail, LANES - count, 1)
    high = value.astype(BF).astype(F32)
    low = pltpu.roll(value - high, count, 1)
    return jnp.where(lane < count, high, jnp.where(lane < 2 * count, low, 0.0))


def call_small(kernel, name, shapes, *args):
    size = sum(4 * math.prod(a.shape) for a in args) + sum(4 * math.prod(s.shape) for s in shapes)
    return pl.pallas_call(
        kernel,
        grid=(1,),
        in_specs=[whole_block(a.shape) for a in args],
        out_specs=[whole_block(s.shape) for s in shapes],
        out_shape=shapes,
        compiler_params=params(2 * size),
        cost_estimate=pl.CostEstimate(flops=size, bytes_accessed=size, transcendentals=0),
        name=name,
    )(*args)


def group_sum_kernel(group, n_got, n_expert, first, own, *refs):
    gots, refs = refs[:n_got], refs[n_got:]
    value = own[...]
    for got in gots:
        value = value + got[...].astype(F32)
    if first:
        width = (value.shape[1] - LANES) // len(group)
        pair = repack(value[:, len(group) * width :], n_expert).astype(BF)
        refs[-1][...] = pair
    else:
        width = value.shape[1] // len(group)
        pair, refs = refs[0][...], refs[1:]
    for at, slot in enumerate(group):
        out = refs[at]
        out[:, :width] = value[:, at * width : (at + 1) * width].astype(out.dtype)
        if slot > 0:
            out[:, width:] = pair


def group_sum(group, own, gots, pair, n_expert, width):
    tokens = own.shape[0]
    shapes = [
        jax.ShapeDtypeStruct((tokens, width + LANES), BF)
        if slot > 0
        else jax.ShapeDtypeStruct((tokens, width), F32)
        for slot in group
    ]
    first = pair is None
    if first:
        shapes.append(jax.ShapeDtypeStruct((tokens, LANES), BF))
    kernel = functools.partial(group_sum_kernel, group, len(gots), n_expert, first)
    out = call_small(kernel, "group_sum", shapes, own, *gots, *([] if first else [pair]))
    return out[: len(group)], (out[-1] if first else pair)


def final_sum_kernel(n_expert, own, pair, ids, *refs):
    fars, (grad, route) = refs[:-2], refs[-2:]
    width = own.shape[1]
    value, tail = own[...], pair[...].astype(F32)
    for far in fars:
        value = value + far[:, :width].astype(F32)
        tail = tail + far[:, width:].astype(F32)
    grad[...] = value.astype(BF)
    tail = tail + pltpu.roll(tail, LANES - n_expert, 1)
    lane = lax.broadcasted_iota(jnp.int32, tail.shape, 1)
    for k in range(route.shape[1]):
        chosen = jnp.logical_and(lane == ids[:, k : k + 1], lane < n_expert)
        route[:, k : k + 1] = jnp.sum(jnp.where(chosen, tail, 0.0), axis=1, keepdims=True)


def final_sum(own, fars, pair, ids, n_expert):
    shapes = [jax.ShapeDtypeStruct(own.shape, BF), jax.ShapeDtypeStruct(ids.shape, F32)]
    kernel = functools.partial(final_sum_kernel, n_expert)
    return call_small(kernel, "final_sum", shapes, own, pair, ids, *fars)


def per_device(
    n_expert,
    n_slice,
    tokens,
    cotangent,
    route_ids,
    route_weights,
    gate_weight,
    up_weight,
    down_weight,
    fisher,
    anchor,
):
    count, width = tokens.shape
    chips = n_expert // 2
    rows = chips * count
    lo = 1 << ((chips.bit_length() - 1) // 2)
    hi = chips // lo
    own_e, own_f = lax.axis_index("expert"), lax.axis_index("ffn")
    place = jnp.stack([own_f, own_e]).astype(jnp.int32)

    def over_expert(value, mask):
        return lax.ppermute(value, "expert", [(i, i ^ mask) for i in range(n_expert)])

    def over_lo(value, mask):
        return over_expert(value, 2 * mask)

    def over_hi(value, mask):
        return over_expert(value, 2 * lo * mask)

    def over_slice(value, mask):
        return lax.ppermute(value, "ffn", [(i, i ^ mask) for i in range(n_slice)])

    def collect(value, send, number, axis):
        return jnp.stack([value] + [send(value, m) for m in range(1, number)], axis=axis)

    named = route_ids[:, :, None] == jnp.arange(LANES, dtype=jnp.int32)[None, None, :]
    route_row = jnp.sum(
        jnp.where(named, route_weights.astype(F32)[:, :, None], 0.0), axis=1
    ).astype(BF)

    together = lax.optimization_barrier
    both = jnp.concatenate([tokens, cotangent], axis=1)
    masks = range(2, n_expert, 2)

    def to_chips(part):
        return [over_expert(part, m) for m in masks]

    def assemble(part, hops):
        return jnp.stack([part] + hops).reshape(rows, -1)

    hops, parts, both = together(
        (to_chips(both), [over_slice(both, s) for s in range(1, 3)], both)
    )
    near = [assemble(both, hops)]
    part = jnp.concatenate([*parts, route_row], axis=1)
    gate, up, down = gate_weight[0], up_weight[0], down_weight[0]
    penalty = fisher[0] * (down.astype(F32) - anchor[0])
    other = [over_expert(after(gate, both), 1)]
    other.append(over_expert(after(up, both), 1))
    hops, more, part, other, near, penalty = together(
        (
            to_chips(part),
            [over_slice(both, s) for s in range(3, n_slice)],
            part,
            other,
            near,
            penalty,
        )
    )
    near.append(assemble(part, hops))
    more_hops = [to_chips(v) for v in more]
    other.append(over_expert(after(down, *other), 1))
    weights = (gate, up, down, *other)
    acc = forward_near(place, *near, weights, width)
    got_near = [over_expert(v, 1) for v in near]
    more_hops, more, acc, got_near = together((more_hops, more, acc, got_near))
    rest = [assemble(v, h) for v, h in zip(more, more_hops)]
    acts, acts_other, route = forward_rest(
        place, rest, weights, acc, near[1], n_expert, width, 3
    )

    got_acts = over_expert(acts_other, 1)
    got_rest = tuple(over_expert(v, 1) for v in rest)
    ready = after(place, *got_rest)
    sources = (*near, *rest, *got_near, *got_rest)
    pieces = [
        tuple(
            ((0 if s == 0 else 1 if s < 3 else s - 1, None, which + 2 * (s == 2), 0),)
            for s in range(n_slice)
        )
        for which in range(2)
    ]
    own_count = len(near) + len(rest)
    pieces = [
        tuple(one + ((one[0][0] + own_count, *one[0][1:3], rows),) for one in side)
        for side in pieces
    ]

    projections = (weights[0], weights[1], weights[3], weights[4])
    slots = list(reversed(range(n_slice)))
    groups = [slots[: n_slice // 2], slots[n_slice // 2 :]]
    parts, late = [], ready
    for group in groups:
        outs = unit_product(
            late, acts, acts_other, projections, group, count, width, None if parts else route
        )
        parts.append(
            (outs[0], [over_expert(v, 2 * (block + 1)) for block, v in enumerate(outs[1:])])
        )
        late = after(late, got_acts)
    sends, pair = group_sum(groups[0], *parts[0], None, n_expert, width)
    fars = [over_slice(v, s) for s, v in zip(groups[0], sends)]
    late = after(place, *sends)
    grad_gate, grad_up = outer_products(late, sources, pieces[0], acts, got_acts, width)
    own, got = parts[1]
    sends, _ = group_sum(groups[1], after(own, grad_gate), got, pair, n_expert, width)
    fars += [over_slice(v, s) for s, v in zip(groups[1], sends) if s > 0]
    late = after(place, *sends)
    (grad_down,) = outer_products(
        late, sources, pieces[1], acts, got_acts, width, penalty
    )
    own = after(sends[-1], grad_down)
    grad_tokens, grad_route = final_sum(own, fars, pair, route_ids, n_expert)
    return (grad_tokens, grad_route, grad_gate[None], grad_up[None], grad_down[None])


def solution(mesh):
    return jax.shard_map(
        functools.partial(per_device, mesh.shape["expert"], mesh.shape["ffn"]),
        mesh=mesh,
        in_specs=(
            P("expert", "ffn"),
            P("expert", "ffn"),
            P("expert", None),
            P("expert", None),
            P("expert", None, "ffn"),
            P("expert", None, "ffn"),
            P("expert", "ffn", None),
            P("expert", "ffn", None),
            P("expert", "ffn", None),
        ),
        out_specs=(
            P("expert", "ffn"),
            P("expert", None),
            P("expert", None, "ffn"),
            P("expert", None, "ffn"),
            P("expert", "ffn", None),
        ),
        check_vma=False,
    )
```

```python
import functools
import math

import jax
import jax.numpy as jnp
from jax import lax
from jax.experimental import pallas as pl
from jax.experimental.pallas import tpu as pltpu
from jax.sharding import PartitionSpec as P

BF = jnp.bfloat16
F32 = jnp.float32
LANES = 128
MIB = 1024 * 1024


def whole_block(shape):
    zeros = (0,) * len(shape)
    return pl.BlockSpec(shape, lambda *_: zeros, pipeline_mode=pl.Buffered(1))


def dot(a, b, a_dim, b_dim):
    return lax.dot_general(a, b, (((a_dim,), (b_dim,)), ((), ())), preferred_element_type=F32)


def after(value, *first):
    return lax.optimization_barrier((value, *first))[0]


def params(need):
    return pltpu.CompilerParams(vmem_limit_bytes=min(need + 12 * MIB, 58 * MIB))


def add_slice(x, dy, weights, before):
    values = []
    for number, weight in enumerate(weights):
        from_dy = number % 3 == 2
        part = dot(dy if from_dy else x, weight[...], 1, 1 if from_dy else 0)
        values.append(part if before is None else part + before[number])
    return values


def near_kernel(own_ref, near_ref, weights, out):
    width = weights[0].shape[0]
    step = pl.program_id(0)
    for at, (ref, base) in enumerate(((own_ref, 0), (near_ref, 0), (near_ref, 2))):

        @pl.when(step == at)
        def _(at=at, ref=ref, base=base):
            x = ref[:, base * width : (base + 1) * width]
            dy = ref[:, (base + 1) * width : (base + 2) * width]
            values = add_slice(x, dy, weights, out if at else None)
            for number in range(6):
                out[number] = values[number]


def forward_kernel(place, own_ref, near_ref, *refs):
    near_kernel(own_ref, near_ref, refs[:6], refs[6])


def rest_kernel(n_expert, slots, place, *refs):
    sources, refs = refs[: 2 * slots], refs[2 * slots :]
    weights, before, route_w = refs[:6], refs[6], refs[7]
    mine, other, route, held = refs[8:]
    units = weights[0].shape[1]
    step = pl.program_id(0)

    for at in range(slots - 1):

        @pl.when(step == at)
        def _(at=at):
            x, dy = sources[2 * at][...], sources[2 * at + 1][...]
            values = add_slice(x, dy, weights, held if at else before)
            for number in range(6):
                held[number] = values[number]

    @pl.when(step == slots - 1)
    def _():
        values = add_slice(
            sources[-2][...], sources[-1][...], weights, held if slots > 1 else before
        )
        lane = lax.broadcasted_iota(jnp.int32, route.shape, 1)
        total = jnp.zeros(route.shape, F32)
        for j, acts in enumerate((mine, other)):
            expert = jnp.bitwise_xor(place[1], j)
            gate_pre, up_pre, back = values[3 * j : 3 * j + 3]
            weight = jnp.sum(
                jnp.where(lane == expert, route_w[...].astype(F32), 0.0), axis=1, keepdims=True
            )
            logistic = jax.nn.sigmoid(gate_pre)
            active = gate_pre * logistic
            hidden = active * up_pre
            route_part = jnp.sum(back * hidden, axis=1, keepdims=True)
            high = route_part.astype(BF).astype(F32)
            total = total + jnp.where(lane == expert, high, 0.0)
            total = total + jnp.where(lane == expert + n_expert, route_part - high, 0.0)
            scaled = weight * back
            acts[:, :units] = (
                scaled * up_pre * logistic * (1.0 + gate_pre * (1.0 - logistic))
            ).astype(BF)
            acts[:, units : 2 * units] = (scaled * active).astype(BF)
            acts[:, 2 * units :] = (weight * hidden).astype(BF)
        route[...] = total.astype(BF)


def column_block(rows, width, column):
    return pl.BlockSpec(
        (rows, width), lambda i, p: (0, column), pipeline_mode=pl.Buffered(1)
    )


def forward_cost(rows, width, units, slots):
    return pl.CostEstimate(
        flops=12 * rows * width * units * slots,
        bytes_accessed=2 * width * (2 * rows + 6 * units) * slots + 24 * rows * units,
        transcendentals=2 * rows * units,
    )


def forward_near(place, own, near, weights, width):
    rows = own.shape[0]
    units = weights[0].shape[1]
    wide = pl.BlockSpec((width, units), lambda i, p: (p[0] ^ i, 0))
    tall = pl.BlockSpec((units, width), lambda i, p: (0, p[0] ^ i))
    return pl.pallas_call(
        forward_kernel,
        grid_spec=pltpu.PrefetchScalarGridSpec(
            num_scalar_prefetch=1,
            grid=(3,),
            in_specs=[whole_block(own.shape), whole_block(near.shape)]
            + [wide, wide, tall] * 2,
            out_specs=whole_block((6, rows, units)),
        ),
        out_shape=jax.ShapeDtypeStruct((6, rows, units), F32),
        compiler_params=params(14 * MIB),
        cost_estimate=forward_cost(rows, width, units, 3),
        name="forward_near",
    )(place, own, near, *weights)


def forward_rest(place, pairs, weights, before, route_w, n_expert, width, done):
    rows = pairs[0].shape[0]
    units = weights[0].shape[1]
    slots = len(pairs)
    wide = pl.BlockSpec((width, units), lambda i, p: (p[0] ^ (i + done), 0))
    tall = pl.BlockSpec((units, width), lambda i, p: (0, p[0] ^ (i + done)))
    return pl.pallas_call(
        functools.partial(rest_kernel, n_expert, slots),
        grid_spec=pltpu.PrefetchScalarGridSpec(
            num_scalar_prefetch=1,
            grid=(slots,),
            in_specs=[column_block(rows, width, column) for column in range(2)] * slots
            + [wide, wide, tall] * 2
            + [whole_block(before.shape), column_block(rows, LANES, 4 * width // LANES)],
            out_specs=[
                whole_block((rows, 3 * units)),
                whole_block((rows, 3 * units)),
                whole_block((rows, LANES)),
            ],
            scratch_shapes=[pltpu.VMEM((6, rows, units), F32)],
        ),
        out_shape=[
            jax.ShapeDtypeStruct((rows, 3 * units), BF),
            jax.ShapeDtypeStruct((rows, 3 * units), BF),
            jax.ShapeDtypeStruct((rows, LANES), BF),
        ],
        compiler_params=params(
            4 * rows * width * slots + 24 * width * units + 120 * rows * units
        ),
        cost_estimate=forward_cost(rows, width, units, slots),
        name="forward_rest",
    )(place, *[p for pair in pairs for p in (pair, pair)], *weights, before, route_w)


def unit_kernel(tokens, slots, with_route, place, mine, other, *refs):
    if with_route:
        route, refs = refs[0], refs[1:]
    weights, outs = refs[:4], refs[4:]
    width, units = weights[0].shape
    step = pl.program_id(0)
    total = None
    for number, weight in enumerate(weights):
        acts = mine if number < 2 else other
        at = (number % 2) * units
        part = dot(acts[:, at : at + units], weight[...], 1, 1)
        total = part if total is None else total + part
    for slot in range(slots):

        @pl.when(step == slot)
        def _(slot=slot):
            for block, out in enumerate(outs):
                rows = pl.ds(block * tokens, tokens)
                value = total[block * tokens : (block + 1) * tokens]
                out[:, slot * width : (slot + 1) * width] = value.astype(out.dtype)
                if with_route and slot == 0:
                    out[:, slots * width :] = route[rows, :].astype(out.dtype)


def unit_product(place, mine, other, weights, group, tokens, width, route=None):
    rows = mine.shape[0]
    units = weights[0].shape[1]
    slots, top = len(group), group[0]
    wide = pl.BlockSpec((width, units), lambda i, p: (p[0] ^ (top - i), 0))
    acts = column_block(rows, 2 * units, 0)
    columns = slots * width + (0 if route is None else LANES)
    shapes = [
        jax.ShapeDtypeStruct((tokens, columns), F32 if block == 0 else BF)
        for block in range(rows // tokens)
    ]
    extra = [] if route is None else [route]
    return pl.pallas_call(
        functools.partial(unit_kernel, tokens, slots, route is not None),
        grid_spec=pltpu.PrefetchScalarGridSpec(
            num_scalar_prefetch=1,
            grid=(slots,),
            in_specs=[acts, acts] + [whole_block(r.shape) for r in extra] + [wide] * 4,
            out_specs=[whole_block(s.shape) for s in shapes],
        ),
        out_shape=shapes,
        compiler_params=params(
            16 * width * units + 16 * rows * units + (8 + 4 * slots) * rows * width
        ),
        cost_estimate=pl.CostEstimate(
            flops=8 * rows * width * units * slots,
            bytes_accessed=8 * width * units * slots + 3 * rows * width * slots,
            transcendentals=0,
        ),
        name="unit_product",
    )(place, mine, other, *extra, *weights)


def outer_kernel(pieces, n_source, rows, down, place, acts, got, *refs):
    n_slice = len(pieces)
    sources, refs = refs[:n_source], refs[n_source:]
    if down:
        penalty, out = refs[:2]
    else:
        gate_out, up_out = refs[:2]
    held, grads, sems = refs[-3:]
    width = held.shape[2]
    units = acts.shape[1] // 3
    step = pl.program_id(0)

    def copies(slot):
        out = []
        for number, (source, index, column, at) in enumerate(pieces[slot]):
            ref = sources[source]
            ref = ref if index is None else ref.at[index]
            out.append(
                pltpu.make_async_copy(
                    ref.at[:, pl.ds(column * width, width)],
                    held.at[slot, pl.ds(at, ref.shape[0])],
                    sems.at[slot, number],
                )
            )
        return out

    @pl.when(step == 0)
    def _():
        for slot in range(n_slice):
            for copy in copies(slot):
                copy.start()
        grads[:rows] = acts[...]
        grads[rows:] = got[...]

    for slot in range(n_slice):

        @pl.when(step == slot)
        def _(slot=slot):
            for copy in copies(slot):
                copy.wait()

    block = held[step]
    if down:
        value = dot(grads[:, 2 * units :], block, 0, 0)
        out[...] = (value + penalty[...]).astype(BF)
    else:
        value = dot(block, grads[:, : 2 * units], 0, 0)
        gate_out[...] = value[:, :units].astype(BF)
        up_out[...] = value[:, units:].astype(BF)


def outer_products(place, sources, pieces, acts, got, width, penalty=None):
    n_slice = len(pieces)
    rows = acts.shape[0]
    units = acts.shape[1] // 3
    full = n_slice * width
    down = penalty is not None
    wide = pl.BlockSpec((width, units), lambda s, p: (p[0] ^ s, 0))
    tall = pl.BlockSpec((units, width), lambda s, p: (0, p[0] ^ s))
    anywhere = pl.BlockSpec(memory_space=pl.ANY)
    return pl.pallas_call(
        functools.partial(outer_kernel, pieces, len(sources), rows, down),
        grid_spec=pltpu.PrefetchScalarGridSpec(
            num_scalar_prefetch=1,
            grid=(n_slice,),
            in_specs=[whole_block(acts.shape), whole_block(got.shape)]
            + [anywhere] * len(sources)
            + [tall] * down,
            out_specs=[tall] if down else [wide, wide],
            scratch_shapes=[
                pltpu.VMEM((n_slice, 2 * rows, width), BF),
                pltpu.VMEM((2 * rows, 3 * units), BF),
                pltpu.SemaphoreType.DMA((n_slice, max(len(p) for p in pieces))),
            ],
        ),
        out_shape=[jax.ShapeDtypeStruct((units, full), BF)]
        if down
        else [jax.ShapeDtypeStruct((full, units), BF)] * 2,
        compiler_params=params(58 * MIB),
        cost_estimate=pl.CostEstimate(
            flops=4 * rows * full * units * (1 if down else 2),
            bytes_accessed=full * (4 * rows + units * (6 if down else 4)),
            transcendentals=0,
        ),
        name="outer_down" if down else "outer_gate_up",
    )(place, acts, got, *sources, *([penalty] if down else []))


def repack(tail, count):
    lane = lax.broadcasted_iota(jnp.int32, tail.shape, 1)
    value = tail + pltpu.roll(tail, LANES - count, 1)
    high = value.astype(BF).astype(F32)
    low = pltpu.roll(value - high, count, 1)
    return jnp.where(lane < count, high, jnp.where(lane < 2 * count, low, 0.0))


def call_small(kernel, name, shapes, *args):
    size = sum(4 * math.prod(a.shape) for a in args) + sum(4 * math.prod(s.shape) for s in shapes)
    return pl.pallas_call(
        kernel,
        grid=(1,),
        in_specs=[whole_block(a.shape) for a in args],
        out_specs=[whole_block(s.shape) for s in shapes],
        out_shape=shapes,
        compiler_params=params(2 * size),
        cost_estimate=pl.CostEstimate(flops=size, bytes_accessed=size, transcendentals=0),
        name=name,
    )(*args)


def group_sum_kernel(group, n_got, n_expert, first, own, *refs):
    gots, refs = refs[:n_got], refs[n_got:]
    value = own[...]
    for got in gots:
        value = value + got[...].astype(F32)
    if first:
        width = (value.shape[1] - LANES) // len(group)
        pair = repack(value[:, len(group) * width :], n_expert).astype(BF)
        refs[-1][...] = pair
    else:
        width = value.shape[1] // len(group)
        pair, refs = refs[0][...], refs[1:]
    for at, slot in enumerate(group):
        out = refs[at]
        out[:, :width] = value[:, at * width : (at + 1) * width].astype(out.dtype)
        if slot > 0:
            out[:, width:] = pair


def group_sum(group, own, gots, pair, n_expert, width):
    tokens = own.shape[0]
    shapes = [
        jax.ShapeDtypeStruct((tokens, width + LANES), BF)
        if slot > 0
        else jax.ShapeDtypeStruct((tokens, width), F32)
        for slot in group
    ]
    first = pair is None
    if first:
        shapes.append(jax.ShapeDtypeStruct((tokens, LANES), BF))
    kernel = functools.partial(group_sum_kernel, group, len(gots), n_expert, first)
    out = call_small(kernel, "group_sum", shapes, own, *gots, *([] if first else [pair]))
    return out[: len(group)], (out[-1] if first else pair)


def final_sum_kernel(n_expert, own, pair, ids, *refs):
    fars, (grad, route) = refs[:-2], refs[-2:]
    width = own.shape[1]
    value, tail = own[...], pair[...].astype(F32)
    for far in fars:
        value = value + far[:, :width].astype(F32)
        tail = tail + far[:, width:].astype(F32)
    grad[...] = value.astype(BF)
    tail = tail + pltpu.roll(tail, LANES - n_expert, 1)
    lane = lax.broadcasted_iota(jnp.int32, tail.shape, 1)
    for k in range(route.shape[1]):
        chosen = jnp.logical_and(lane == ids[:, k : k + 1], lane < n_expert)
        route[:, k : k + 1] = jnp.sum(jnp.where(chosen, tail, 0.0), axis=1, keepdims=True)


def final_sum(own, fars, pair, ids, n_expert):
    shapes = [jax.ShapeDtypeStruct(own.shape, BF), jax.ShapeDtypeStruct(ids.shape, F32)]
    kernel = functools.partial(final_sum_kernel, n_expert)
    return call_small(kernel, "final_sum", shapes, own, pair, ids, *fars)


def per_device(
    n_expert,
    n_slice,
    tokens,
    cotangent,
    route_ids,
    route_weights,
    gate_weight,
    up_weight,
    down_weight,
    fisher,
    anchor,
):
    count, width = tokens.shape
    chips = n_expert // 2
    rows = chips * count
    lo = 1 << ((chips.bit_length() - 1) // 2)
    hi = chips // lo
    own_e, own_f = lax.axis_index("expert"), lax.axis_index("ffn")
    place = jnp.stack([own_f, own_e]).astype(jnp.int32)

    def over_expert(value, mask):
        return lax.ppermute(value, "expert", [(i, i ^ mask) for i in range(n_expert)])

    def over_lo(value, mask):
        return over_expert(value, 2 * mask)

    def over_hi(value, mask):
        return over_expert(value, 2 * lo * mask)

    def over_slice(value, mask):
        return lax.ppermute(value, "ffn", [(i, i ^ mask) for i in range(n_slice)])

    def collect(value, send, number, axis):
        return jnp.stack([value] + [send(value, m) for m in range(1, number)], axis=axis)

    named = route_ids[:, :, None] == jnp.arange(LANES, dtype=jnp.int32)[None, None, :]
    route_row = jnp.sum(
        jnp.where(named, route_weights.astype(F32)[:, :, None], 0.0), axis=1
    ).astype(BF)

    together = lax.optimization_barrier
    both = jnp.concatenate([tokens, cotangent], axis=1)
    masks = range(2, n_expert, 2)

    def to_chips(part, before=()):
        near = [over_expert(part, m) for m in masks[:-1]]
        return near + [over_expert(after(part, *before) if before else part, masks[-1])]

    def assemble(part, hops):
        return jnp.stack([part] + hops).reshape(rows, -1)

    parts = [over_slice(both, s) for s in range(2, 0, -1)][::-1]
    hops, parts, both = together((to_chips(both), parts, both))
    near = [assemble(both, hops)]
    part = jnp.concatenate([*parts, route_row], axis=1)
    gate, up, down = gate_weight[0], up_weight[0], down_weight[0]
    penalty = fisher[0] * (down.astype(F32) - anchor[0])
    other = [over_expert(after(gate, both), 1)]
    other.append(over_expert(after(up, both), 1))
    hops, more, part, other, near, penalty = together(
        (
            to_chips(part, other),
            [over_slice(both, s) for s in range(3, n_slice)],
            part,
            other,
            near,
            penalty,
        )
    )
    near.append(assemble(part, hops))
    more_hops = [to_chips(v) for v in more]
    other.append(over_expert(after(down, *other), 1))
    weights = (gate, up, down, *other)
    acc = forward_near(place, *near, weights, width)
    got_near = [over_expert(v, 1) for v in near]
    more_hops, more, acc, got_near = together((more_hops, more, acc, got_near))
    rest = [assemble(v, h) for v, h in zip(more, more_hops)]
    acts, acts_other, route = forward_rest(
        place, rest, weights, acc, near[1], n_expert, width, 3
    )

    got_acts = over_expert(acts_other, 1)
    got_rest = tuple(over_expert(v, 1) for v in rest)
    ready = after(place, *got_rest)
    sources = (*near, *rest, *got_near, *got_rest)
    pieces = [
        tuple(
            ((0 if s == 0 else 1 if s < 3 else s - 1, None, which + 2 * (s == 2), 0),)
            for s in range(n_slice)
        )
        for which in range(2)
    ]
    own_count = len(near) + len(rest)
    pieces = [
        tuple(one + ((one[0][0] + own_count, *one[0][1:3], rows),) for one in side)
        for side in pieces
    ]

    projections = (weights[0], weights[1], weights[3], weights[4])
    slots = list(reversed(range(n_slice)))
    groups = [slots[: n_slice // 2], slots[n_slice // 2 :]]
    parts, late = [], ready
    for group in groups:
        outs = unit_product(
            late, acts, acts_other, projections, group, count, width, None if parts else route
        )
        parts.append(
            (outs[0], [over_expert(v, 2 * (block + 1)) for block, v in enumerate(outs[1:])])
        )
        late = after(late, got_acts)
    late = after(place, parts[1][0])
    (grad_down,) = outer_products(late, sources, pieces[1], acts, got_acts, width, penalty)
    own, got = parts[0]
    sends, pair = group_sum(groups[0], after(own, grad_down), got, None, n_expert, width)
    fars = [over_slice(v, s) for s, v in zip(groups[0], sends)]
    own, got = parts[1]
    sends, _ = group_sum(groups[1], after(own, *sends), got, pair, n_expert, width)
    fars += [over_slice(v, s) for s, v in zip(groups[1], sends) if s > 0]
    late = after(place, *sends)
    grad_gate, grad_up = outer_products(late, sources, pieces[0], acts, got_acts, width)
    own = after(sends[-1], grad_gate)
    grad_tokens, grad_route = final_sum(own, fars, pair, route_ids, n_expert)
    return (grad_tokens, grad_route, grad_gate[None], grad_up[None], grad_down[None])


def solution(mesh):
    return jax.shard_map(
        functools.partial(per_device, mesh.shape["expert"], mesh.shape["ffn"]),
        mesh=mesh,
        in_specs=(
            P("expert", "ffn"),
            P("expert", "ffn"),
            P("expert", None),
            P("expert", None),
            P("expert", None, "ffn"),
            P("expert", None, "ffn"),
            P("expert", "ffn", None),
            P("expert", "ffn", None),
            P("expert", "ffn", None),
        ),
        out_specs=(
            P("expert", "ffn"),
            P("expert", None),
            P("expert", None, "ffn"),
            P("expert", None, "ffn"),
            P("expert", "ffn", None),
        ),
        check_vma=False,
    )
```

```python
import functools
import math

import jax
import jax.numpy as jnp
from jax import lax
from jax.experimental import pallas as pl
from jax.experimental.pallas import tpu as pltpu
from jax.sharding import PartitionSpec as P

BF = jnp.bfloat16
F32 = jnp.float32
LANES = 128
MIB = 1024 * 1024


def whole_block(shape):
    zeros = (0,) * len(shape)
    return pl.BlockSpec(shape, lambda *_: zeros, pipeline_mode=pl.Buffered(1))


def dot(a, b, a_dim, b_dim):
    return lax.dot_general(a, b, (((a_dim,), (b_dim,)), ((), ())), preferred_element_type=F32)


def after(value, *first):
    return lax.optimization_barrier((value, *first))[0]


def params(need):
    return pltpu.CompilerParams(vmem_limit_bytes=min(need + 12 * MIB, 58 * MIB))


def add_slice(x, dy, weights, before):
    values = []
    for number, weight in enumerate(weights):
        from_dy = number % 3 == 2
        part = dot(dy if from_dy else x, weight[...], 1, 1 if from_dy else 0)
        values.append(part if before is None else part + before[number])
    return values


def near_kernel(own_ref, near_ref, weights, out):
    width = weights[0].shape[0]
    step = pl.program_id(0)
    for at, (ref, base) in enumerate(((own_ref, 0), (near_ref, 0), (near_ref, 2))):

        @pl.when(step == at)
        def _(at=at, ref=ref, base=base):
            x = ref[:, base * width : (base + 1) * width]
            dy = ref[:, (base + 1) * width : (base + 2) * width]
            values = add_slice(x, dy, weights, out if at else None)
            for number in range(6):
                out[number] = values[number]


def forward_kernel(place, own_ref, near_ref, *refs):
    near_kernel(own_ref, near_ref, refs[:6], refs[6])


def rest_kernel(n_expert, slots, place, *refs):
    sources, refs = refs[: 2 * slots], refs[2 * slots :]
    weights, before, route_w = refs[:6], refs[6], refs[7]
    mine, other, route, held = refs[8:]
    units = weights[0].shape[1]
    step = pl.program_id(0)

    for at in range(slots - 1):

        @pl.when(step == at)
        def _(at=at):
            x, dy = sources[2 * at][...], sources[2 * at + 1][...]
            values = add_slice(x, dy, weights, held if at else before)
            for number in range(6):
                held[number] = values[number]

    @pl.when(step == slots - 1)
    def _():
        values = add_slice(
            sources[-2][...], sources[-1][...], weights, held if slots > 1 else before
        )
        lane = lax.broadcasted_iota(jnp.int32, route.shape, 1)
        total = jnp.zeros(route.shape, F32)
        for j, acts in enumerate((mine, other)):
            expert = jnp.bitwise_xor(place[1], j)
            gate_pre, up_pre, back = values[3 * j : 3 * j + 3]
            weight = jnp.sum(
                jnp.where(lane == expert, route_w[...].astype(F32), 0.0), axis=1, keepdims=True
            )
            logistic = jax.nn.sigmoid(gate_pre)
            active = gate_pre * logistic
            hidden = active * up_pre
            route_part = jnp.sum(back * hidden, axis=1, keepdims=True)
            high = route_part.astype(BF).astype(F32)
            total = total + jnp.where(lane == expert, high, 0.0)
            total = total + jnp.where(lane == expert + n_expert, route_part - high, 0.0)
            scaled = weight * back
            acts[:, :units] = (
                scaled * up_pre * logistic * (1.0 + gate_pre * (1.0 - logistic))
            ).astype(BF)
            acts[:, units : 2 * units] = (scaled * active).astype(BF)
            acts[:, 2 * units :] = (weight * hidden).astype(BF)
        route[...] = total.astype(BF)


def column_block(rows, width, column):
    return pl.BlockSpec(
        (rows, width), lambda i, p: (0, column), pipeline_mode=pl.Buffered(1)
    )


def forward_cost(rows, width, units, slots):
    return pl.CostEstimate(
        flops=12 * rows * width * units * slots,
        bytes_accessed=2 * width * (2 * rows + 6 * units) * slots + 24 * rows * units,
        transcendentals=2 * rows * units,
    )


def forward_near(place, own, near, weights, width):
    rows = own.shape[0]
    units = weights[0].shape[1]
    wide = pl.BlockSpec((width, units), lambda i, p: (p[0] ^ i, 0))
    tall = pl.BlockSpec((units, width), lambda i, p: (0, p[0] ^ i))
    return pl.pallas_call(
        forward_kernel,
        grid_spec=pltpu.PrefetchScalarGridSpec(
            num_scalar_prefetch=1,
            grid=(3,),
            in_specs=[whole_block(own.shape), whole_block(near.shape)]
            + [wide, wide, tall] * 2,
            out_specs=whole_block((6, rows, units)),
        ),
        out_shape=jax.ShapeDtypeStruct((6, rows, units), F32),
        compiler_params=params(14 * MIB),
        cost_estimate=forward_cost(rows, width, units, 3),
        name="forward_near",
    )(place, own, near, *weights)


def forward_rest(place, pairs, weights, before, route_w, n_expert, width, done):
    rows = pairs[0].shape[0]
    units = weights[0].shape[1]
    slots = len(pairs)
    wide = pl.BlockSpec((width, units), lambda i, p: (p[0] ^ (i + done), 0))
    tall = pl.BlockSpec((units, width), lambda i, p: (0, p[0] ^ (i + done)))
    return pl.pallas_call(
        functools.partial(rest_kernel, n_expert, slots),
        grid_spec=pltpu.PrefetchScalarGridSpec(
            num_scalar_prefetch=1,
            grid=(slots,),
            in_specs=[column_block(rows, width, column) for column in range(2)] * slots
            + [wide, wide, tall] * 2
            + [whole_block(before.shape), column_block(rows, LANES, 4 * width // LANES)],
            out_specs=[
                whole_block((rows, 3 * units)),
                whole_block((rows, 3 * units)),
                whole_block((rows, LANES)),
            ],
            scratch_shapes=[pltpu.VMEM((6, rows, units), F32)],
        ),
        out_shape=[
            jax.ShapeDtypeStruct((rows, 3 * units), BF),
            jax.ShapeDtypeStruct((rows, 3 * units), BF),
            jax.ShapeDtypeStruct((rows, LANES), BF),
        ],
        compiler_params=params(
            4 * rows * width * slots + 24 * width * units + 120 * rows * units
        ),
        cost_estimate=forward_cost(rows, width, units, slots),
        name="forward_rest",
    )(place, *[p for pair in pairs for p in (pair, pair)], *weights, before, route_w)


def unit_kernel(tokens, slots, with_route, place, mine, other, *refs):
    if with_route:
        route, refs = refs[0], refs[1:]
    weights, outs = refs[:4], refs[4:]
    width, units = weights[0].shape
    step = pl.program_id(0)
    total = None
    for number, weight in enumerate(weights):
        acts = mine if number < 2 else other
        at = (number % 2) * units
        part = dot(acts[:, at : at + units], weight[...], 1, 1)
        total = part if total is None else total + part
    for slot in range(slots):

        @pl.when(step == slot)
        def _(slot=slot):
            for block, out in enumerate(outs):
                rows = pl.ds(block * tokens, tokens)
                value = total[block * tokens : (block + 1) * tokens]
                out[:, slot * width : (slot + 1) * width] = value.astype(out.dtype)
                if with_route and slot == 0:
                    out[:, slots * width :] = route[rows, :].astype(out.dtype)


def unit_product(place, mine, other, weights, group, tokens, width, route=None):
    rows = mine.shape[0]
    units = weights[0].shape[1]
    slots, top = len(group), group[0]
    wide = pl.BlockSpec((width, units), lambda i, p: (p[0] ^ (top - i), 0))
    acts = column_block(rows, 2 * units, 0)
    columns = slots * width + (0 if route is None else LANES)
    shapes = [
        jax.ShapeDtypeStruct((tokens, columns), F32 if block == 0 else BF)
        for block in range(rows // tokens)
    ]
    extra = [] if route is None else [route]
    return pl.pallas_call(
        functools.partial(unit_kernel, tokens, slots, route is not None),
        grid_spec=pltpu.PrefetchScalarGridSpec(
            num_scalar_prefetch=1,
            grid=(slots,),
            in_specs=[acts, acts] + [whole_block(r.shape) for r in extra] + [wide] * 4,
            out_specs=[whole_block(s.shape) for s in shapes],
        ),
        out_shape=shapes,
        compiler_params=params(
            16 * width * units + 16 * rows * units + (8 + 4 * slots) * rows * width
        ),
        cost_estimate=pl.CostEstimate(
            flops=8 * rows * width * units * slots,
            bytes_accessed=8 * width * units * slots + 3 * rows * width * slots,
            transcendentals=0,
        ),
        name="unit_product",
    )(place, mine, other, *extra, *weights)


def outer_kernel(pieces, n_source, rows, down, place, acts, got, *refs):
    n_slice = len(pieces)
    sources, refs = refs[:n_source], refs[n_source:]
    if down:
        penalty, out = refs[:2]
    else:
        gate_out, up_out = refs[:2]
    held, grads, sems = refs[-3:]
    width = held.shape[2]
    units = acts.shape[1] // 3
    step = pl.program_id(0)

    def copies(slot):
        out = []
        for number, (source, index, column, at) in enumerate(pieces[slot]):
            ref = sources[source]
            ref = ref if index is None else ref.at[index]
            out.append(
                pltpu.make_async_copy(
                    ref.at[:, pl.ds(column * width, width)],
                    held.at[slot, pl.ds(at, ref.shape[0])],
                    sems.at[slot, number],
                )
            )
        return out

    @pl.when(step == 0)
    def _():
        for slot in range(n_slice):
            for copy in copies(slot):
                copy.start()
        grads[:rows] = acts[...]
        grads[rows:] = got[...]

    for slot in range(n_slice):

        @pl.when(step == slot)
        def _(slot=slot):
            for copy in copies(slot):
                copy.wait()

    block = held[step]
    if down:
        value = dot(grads[:, 2 * units :], block, 0, 0)
        out[...] = (value + penalty[...]).astype(BF)
    else:
        value = dot(block, grads[:, : 2 * units], 0, 0)
        gate_out[...] = value[:, :units].astype(BF)
        up_out[...] = value[:, units:].astype(BF)


def outer_products(place, sources, pieces, acts, got, width, penalty=None):
    n_slice = len(pieces)
    rows = acts.shape[0]
    units = acts.shape[1] // 3
    full = n_slice * width
    down = penalty is not None
    wide = pl.BlockSpec((width, units), lambda s, p: (p[0] ^ s, 0))
    tall = pl.BlockSpec((units, width), lambda s, p: (0, p[0] ^ s))
    anywhere = pl.BlockSpec(memory_space=pl.ANY)
    return pl.pallas_call(
        functools.partial(outer_kernel, pieces, len(sources), rows, down),
        grid_spec=pltpu.PrefetchScalarGridSpec(
            num_scalar_prefetch=1,
            grid=(n_slice,),
            in_specs=[whole_block(acts.shape), whole_block(got.shape)]
            + [anywhere] * len(sources)
            + [tall] * down,
            out_specs=[tall] if down else [wide, wide],
            scratch_shapes=[
                pltpu.VMEM((n_slice, 2 * rows, width), BF),
                pltpu.VMEM((2 * rows, 3 * units), BF),
                pltpu.SemaphoreType.DMA((n_slice, max(len(p) for p in pieces))),
            ],
        ),
        out_shape=[jax.ShapeDtypeStruct((units, full), BF)]
        if down
        else [jax.ShapeDtypeStruct((full, units), BF)] * 2,
        compiler_params=params(58 * MIB),
        cost_estimate=pl.CostEstimate(
            flops=4 * rows * full * units * (1 if down else 2),
            bytes_accessed=full * (4 * rows + units * (6 if down else 4)),
            transcendentals=0,
        ),
        name="outer_down" if down else "outer_gate_up",
    )(place, acts, got, *sources, *([penalty] if down else []))


def repack(tail, count):
    lane = lax.broadcasted_iota(jnp.int32, tail.shape, 1)
    value = tail + pltpu.roll(tail, LANES - count, 1)
    high = value.astype(BF).astype(F32)
    low = pltpu.roll(value - high, count, 1)
    return jnp.where(lane < count, high, jnp.where(lane < 2 * count, low, 0.0))


def call_small(kernel, name, shapes, *args):
    size = sum(4 * math.prod(a.shape) for a in args) + sum(4 * math.prod(s.shape) for s in shapes)
    return pl.pallas_call(
        kernel,
        grid=(1,),
        in_specs=[whole_block(a.shape) for a in args],
        out_specs=[whole_block(s.shape) for s in shapes],
        out_shape=shapes,
        compiler_params=params(2 * size),
        cost_estimate=pl.CostEstimate(flops=size, bytes_accessed=size, transcendentals=0),
        name=name,
    )(*args)


def join_kernel(left, right, out):
    width = left.shape[1]
    out[:, :width] = left[...]
    out[:, width:] = right[...]


def group_sum_kernel(group, n_got, n_expert, first, own, *refs):
    gots, refs = refs[:n_got], refs[n_got:]
    value = own[...]
    for got in gots:
        value = value + got[...].astype(F32)
    if first:
        width = (value.shape[1] - LANES) // len(group)
        pair = repack(value[:, len(group) * width :], n_expert).astype(BF)
        refs[-1][...] = pair
    else:
        width = value.shape[1] // len(group)
        pair, refs = refs[0][...], refs[1:]
    for at, slot in enumerate(group):
        out = refs[at]
        out[:, :width] = value[:, at * width : (at + 1) * width].astype(out.dtype)
        if slot > 0:
            out[:, width:] = pair


def group_sum(group, own, gots, pair, n_expert, width):
    tokens = own.shape[0]
    shapes = [
        jax.ShapeDtypeStruct((tokens, width + LANES), BF)
        if slot > 0
        else jax.ShapeDtypeStruct((tokens, width), F32)
        for slot in group
    ]
    first = pair is None
    if first:
        shapes.append(jax.ShapeDtypeStruct((tokens, LANES), BF))
    kernel = functools.partial(group_sum_kernel, group, len(gots), n_expert, first)
    out = call_small(kernel, "group_sum", shapes, own, *gots, *([] if first else [pair]))
    return out[: len(group)], (out[-1] if first else pair)


def final_sum_kernel(n_expert, own, pair, ids, *refs):
    fars, (grad, route) = refs[:-2], refs[-2:]
    width = own.shape[1]
    value, tail = own[...], pair[...].astype(F32)
    for far in fars:
        value = value + far[:, :width].astype(F32)
        tail = tail + far[:, width:].astype(F32)
    grad[...] = value.astype(BF)
    tail = tail + pltpu.roll(tail, LANES - n_expert, 1)
    lane = lax.broadcasted_iota(jnp.int32, tail.shape, 1)
    for k in range(route.shape[1]):
        chosen = jnp.logical_and(lane == ids[:, k : k + 1], lane < n_expert)
        route[:, k : k + 1] = jnp.sum(jnp.where(chosen, tail, 0.0), axis=1, keepdims=True)


def final_sum(own, fars, pair, ids, n_expert):
    shapes = [jax.ShapeDtypeStruct(own.shape, BF), jax.ShapeDtypeStruct(ids.shape, F32)]
    kernel = functools.partial(final_sum_kernel, n_expert)
    return call_small(kernel, "final_sum", shapes, own, pair, ids, *fars)


def per_device(
    n_expert,
    n_slice,
    tokens,
    cotangent,
    route_ids,
    route_weights,
    gate_weight,
    up_weight,
    down_weight,
    fisher,
    anchor,
):
    count, width = tokens.shape
    chips = n_expert // 2
    rows = chips * count
    lo = 1 << ((chips.bit_length() - 1) // 2)
    hi = chips // lo
    own_e, own_f = lax.axis_index("expert"), lax.axis_index("ffn")
    place = jnp.stack([own_f, own_e]).astype(jnp.int32)

    def over_expert(value, mask):
        return lax.ppermute(value, "expert", [(i, i ^ mask) for i in range(n_expert)])

    def over_lo(value, mask):
        return over_expert(value, 2 * mask)

    def over_hi(value, mask):
        return over_expert(value, 2 * lo * mask)

    def over_slice(value, mask):
        return lax.ppermute(value, "ffn", [(i, i ^ mask) for i in range(n_slice)])

    def collect(value, send, number, axis):
        return jnp.stack([value] + [send(value, m) for m in range(1, number)], axis=axis)

    named = route_ids[:, :, None] == jnp.arange(LANES, dtype=jnp.int32)[None, None, :]
    route_row = jnp.sum(
        jnp.where(named, route_weights.astype(F32)[:, :, None], 0.0), axis=1
    ).astype(BF)

    together = lax.optimization_barrier
    joined = jax.ShapeDtypeStruct((count, 2 * width), BF)
    (both,) = call_small(join_kernel, "join", [joined], tokens, cotangent)
    masks = range(2, n_expert, 2)

    def to_chips(part, before=()):
        near = [over_expert(part, m) for m in masks[:-1]]
        return near + [over_expert(after(part, *before) if before else part, masks[-1])]

    def assemble(part, hops):
        return jnp.stack([part] + hops).reshape(rows, -1)

    parts = [over_slice(both, s) for s in range(2, 0, -1)][::-1]
    hops, parts, both = together((to_chips(both), parts, both))
    near = [assemble(both, hops)]
    part = jnp.concatenate([*parts, route_row], axis=1)
    gate, up, down = gate_weight[0], up_weight[0], down_weight[0]
    penalty = fisher[0] * (down.astype(F32) - anchor[0])
    other = [over_expert(after(gate, both), 1)]
    other.append(over_expert(after(up, both), 1))
    hops, more, part, other, near, penalty = together(
        (
            to_chips(part, other),
            [over_slice(both, s) for s in range(3, n_slice)],
            part,
            other,
            near,
            penalty,
        )
    )
    near.append(assemble(part, hops))
    more_hops = [to_chips(v) for v in more]
    other.append(over_expert(after(down, *other), 1))
    weights = (gate, up, down, *other)
    acc = forward_near(place, *near, weights, width)
    got_near = [over_expert(v, 1) for v in near]
    more_hops, more, acc, got_near = together((more_hops, more, acc, got_near))
    rest = [assemble(v, h) for v, h in zip(more, more_hops)]
    acts, acts_other, route = forward_rest(
        place, rest, weights, acc, near[1], n_expert, width, 3
    )

    got_acts = over_expert(acts_other, 1)
    got_rest = tuple(over_expert(v, 1) for v in rest)
    ready = after(place, *got_rest)
    sources = (*near, *rest, *got_near, *got_rest)
    pieces = [
        tuple(
            ((0 if s == 0 else 1 if s < 3 else s - 1, None, which + 2 * (s == 2), 0),)
            for s in range(n_slice)
        )
        for which in range(2)
    ]
    own_count = len(near) + len(rest)
    pieces = [
        tuple(one + ((one[0][0] + own_count, *one[0][1:3], rows),) for one in side)
        for side in pieces
    ]

    projections = (weights[0], weights[1], weights[3], weights[4])
    slots = list(reversed(range(n_slice)))
    groups = [slots[: n_slice // 2], slots[n_slice // 2 :]]
    parts, late = [], ready
    for group in groups:
        outs = unit_product(
            late, acts, acts_other, projections, group, count, width, None if parts else route
        )
        parts.append(
            (outs[0], [over_expert(v, 2 * (block + 1)) for block, v in enumerate(outs[1:])])
        )
        late = after(late, got_acts)
    late = after(place, parts[1][0])
    (grad_down,) = outer_products(late, sources, pieces[1], acts, got_acts, width, penalty)
    own, got = parts[0]
    sends, pair = group_sum(groups[0], after(own, grad_down), got, None, n_expert, width)
    fars = [over_slice(v, s) for s, v in zip(groups[0], sends)]
    own, got = parts[1]
    sends, _ = group_sum(groups[1], after(own, *sends), got, pair, n_expert, width)
    fars += [over_slice(v, s) for s, v in zip(groups[1], sends) if s > 0]
    late = after(place, *sends)
    grad_gate, grad_up = outer_products(late, sources, pieces[0], acts, got_acts, width)
    own = after(sends[-1], grad_gate)
    grad_tokens, grad_route = final_sum(own, fars, pair, route_ids, n_expert)
    return (grad_tokens, grad_route, grad_gate[None], grad_up[None], grad_down[None])


def solution(mesh):
    return jax.shard_map(
        functools.partial(per_device, mesh.shape["expert"], mesh.shape["ffn"]),
        mesh=mesh,
        in_specs=(
            P("expert", "ffn"),
            P("expert", "ffn"),
            P("expert", None),
            P("expert", None),
            P("expert", None, "ffn"),
            P("expert", None, "ffn"),
            P("expert", "ffn", None),
            P("expert", "ffn", None),
            P("expert", "ffn", None),
        ),
        out_specs=(
            P("expert", "ffn"),
            P("expert", None),
            P("expert", None, "ffn"),
            P("expert", None, "ffn"),
            P("expert", "ffn", None),
        ),
        check_vma=False,
    )
```
